512 devices in a mesh: section: 4 (over z_lo), dp: 16 (over z_hi, y), mp: 8 (over x, core).
Axes of the slice: x: 4, y: 8, z: 8 (z_hi: 2, z_lo: 4; z = z_hi * 4 + z_lo), core: 2. Of those that a mesh axis runs over, the one named last changes fastest.
Arguments:
- passage_tokens: bfloat16 [128, 128, 2048], P(('section', 'dp'), None, 'mp'), may hold values from -6 to 6
- query_tokens: bfloat16 [256, 32, 2048], P(('section', 'dp'), None, 'mp'), may hold values from -6 to 6
- norm_gain: bfloat16 [2048], P('mp'), may hold values from 0.5 to 1.5
- w_gate: bfloat16 [2048, 5120], P('dp', 'mp'), may hold values from -0.125 to 0.125
- w_up: bfloat16 [2048, 5120], P('dp', 'mp'), may hold values from -0.125 to 0.125
- w_down: bfloat16 [5120, 2048], P('mp', 'dp'), may hold values from -0.078125 to 0.078125
- old_head: bfloat16 [2048, 768], P('mp'), may hold values from -0.125 to 0.125
- new_head: bfloat16 [2048, 768], P('mp'), may hold values from -0.125 to 0.125
- stale_index: bfloat16 [131072, 768], P(('section', 'dp'), 'mp'), may hold values from -6 to 6
- neg_owner: int32 [256, 8], P(('section', 'dp')), may hold values from 0 to 63, all different within a row; in each aligned block of 4 rows (0 to 3, 4 to 7, ...) at most 2 rows name the same one
- neg_row: int32 [256, 8], P(('section', 'dp')), may hold values from 0 to 2047
- pos_slot: int32 [256], P(('section', 'dp')), may hold values from 0 to 1
Outputs:
- refreshed: bfloat16 [128, 768], P(('section', 'dp'), 'mp')
- losses: float32 [256], P(('section', 'dp'))
- head_grad: float32 [2048, 768], P('mp', 'dp')
The draws below stay inside these ranges and needn't reach their ends.
Inputs may be any that keep to these rules, and one draw needn't show every extreme that they name: `neg_owner`: each query names 8 different index shards; the 4 queries of one shard name one index shard at most 2 times.
All inputs are finite; a program needn't handle non-finite values.
Results may differ from the reference program's by a relative error of at most 0.029.
Values may be sent and summed in bfloat16 or wider, within the bound.
No kernel may reach another device: no remote copies, remote signals or barrier semaphores. Data moves between devices by JAX's collectives and lax.ppermute only.
A program may use at most 64 MiB of HBM per device.

```python
import math
import jax
import jax.numpy as jnp
import numpy as np
from jax import lax

D = 2048
FF = 5120
E = 768
L = 128
LQ = 32
K = 8
P_DEV = 2
Q_DEV = 4
INDEX_DEV = 2048
OWNERS = 64
CAP = 2
PASSAGES = 128
QUERIES = 256
INDEX = 131072


def with_ends(drawn, own_key, low, top_value):
    dims = drawn.shape
    spot = [jax.random.randint(jax.random.fold_in(own_key, axis), (), 0, dims[axis]) for axis in range(len(dims))]
    drawn = drawn.at[tuple(spot)].set(low)
    longest = dims.index(max(dims))
    spot[longest] = (spot[longest] + 1) % dims[longest]
    return drawn.at[tuple(spot)].set(top_value)


def steps_of(stream_key, shape, split, least, high):
    level = 1.0
    for dim, shards_of in split:
        draws = jax.random.uniform(jax.random.fold_in(jax.random.fold_in(stream_key, 6), dim), (shards_of,), jnp.float32, least / len(split), high / len(split))
        level = level * jnp.repeat(jnp.exp(draws), shape[dim] // shards_of).reshape((-1,) + (1,) * (len(shape) - 1 - dim))
    return level


def routed_block(stream_key, own, number, rows, count, top, bound, skew):
    order = jax.random.permutation(stream_key, count)
    crowded, ordinary = portions_of(count, rows * top, bound, skew, True), portions_of(count, rows * top, bound, skew, False)
    places = jnp.arange(count)

    def named(sizes, rotation):
        used = int((sizes > 0).sum())
        fixed = max(1, used // 4)
        passed = fixed + (places - fixed + rotation * (used - fixed)) % max(1, count - fixed)
        return jnp.zeros((count,), jnp.int32).at[order[jnp.where(places < fixed, places, passed)]].set(jnp.asarray(sizes, jnp.int32))

    sizes = jnp.where(number % 4 == 0, named(crowded, number // 4), named(ordinary, number - number // 4 - 1))
    mixed = jax.random.permutation(jax.random.fold_in(own, 3), count)
    giver, sink = mixed[0:count // 2 * 2:2], mixed[1:count // 2 * 2:2]
    margin = jnp.minimum(sizes[giver] - 1, bound - sizes[sink]) // 2
    margin = jnp.where((giver == order[0]) | (sink == order[0]) | (sizes[sink] == 0), 0, jnp.maximum(margin, 0))
    passed = jax.random.randint(jax.random.fold_in(own, 4), (count // 2,), 0, 1 << 20) % (margin + 1)
    sizes = sizes.at[giver].add(-passed).at[sink].add(passed)
    members = jnp.searchsorted(jnp.cumsum(sizes), jnp.arange(rows * top), side="right").astype(jnp.int32)
    grid = members.reshape(top, rows).T
    grid = grid[jax.random.permutation(jax.random.fold_in(own, 1), rows)]
    rotation = jax.random.randint(jax.random.fold_in(own, 2), (rows, 1), 0, top)
    return jnp.take_along_axis(grid, (jnp.arange(top)[None, :] + rotation) % top, axis=1)


def portions_of(number_of, total, bound, slope, full):
    weights = [(1 << 20) // math.isqrt(grade ** slope) + 1 for grade in range(1, number_of + 1)]
    largest = bound if full else min(bound, max(-(-total // number_of), total * weights[0] // sum(weights)))
    least = 1 if total - largest >= number_of - 1 else 0
    given, spare = [largest] + [least] * (number_of - 1), total - largest - least * (number_of - 1)
    while spare > 0:
        free = [i for i in range(1, number_of) if given[i] < largest] or [i for i in range(1, number_of) if given[i] < bound]
        whole, left = sum([weights[i] for i in free]), spare
        for i in free:
            more = min(bound - given[i], max(1, left * weights[i] // whole), spare)
            given[i] = given[i] + more
            spare = spare - more
    return np.array(given)


def centred(stream_key, extent, deviation, limit, split=(), kind=jnp.bfloat16):
    result = jax.random.normal(stream_key, extent, jnp.float32) * deviation
    if len(split) > 0:
        result = steps_of(stream_key, extent, split, -0.22, 0.18) * result
    return jnp.clip(result, min=-limit, max=limit).astype(kind)


def setup_inputs(seed: int = 0) -> dict:
    arg_keys = jax.random.split(jax.random.key(seed), 13)
    passage_tokens = centred(arg_keys[0], (PASSAGES, L, D), 1.0, 6.0, ((0, 64), (2, 8)))
    query_tokens = centred(arg_keys[1], (QUERIES, LQ, D), 1.0, 6.0, ((0, 64), (2, 8)))
    norm_gain = jnp.clip(1.0 + 0.1 * jax.random.normal(arg_keys[2], (D,), jnp.float32), 0.5, 1.5).astype(jnp.bfloat16)
    w_gate = centred(arg_keys[3], (D, FF), D ** -0.5, 0.125, ((0, 16), (1, 8)))
    w_up = centred(arg_keys[4], (D, FF), D ** -0.5, 0.125, ((0, 16), (1, 8)))
    w_down = centred(arg_keys[5], (FF, D), FF ** -0.5, 0.078125, ((0, 8), (1, 16)))
    old_head = centred(arg_keys[6], (D, E), D ** -0.5, 0.125, ((0, 8),))
    new_head = centred(arg_keys[7], (D, E), D ** -0.5, 0.125, ((0, 8),))
    stale_index = centred(arg_keys[8], (INDEX, E), 1.0, 6.0, ((0, 64), (1, 8)))
    neg_owner_keys = jax.random.split(jax.random.fold_in(arg_keys[9], 1), QUERIES // Q_DEV)
    neg_owner_turns = jax.random.permutation(jax.random.fold_in(arg_keys[9], 3), QUERIES // Q_DEV)
    neg_owner = jax.vmap(lambda own, number: routed_block(jax.random.fold_in(arg_keys[9], 2), own, number, Q_DEV, OWNERS, K, CAP, 2))(neg_owner_keys, neg_owner_turns).reshape((QUERIES, K))
    neg_row = with_ends(jax.random.randint(arg_keys[10], (QUERIES, K), 0, INDEX_DEV), jax.random.fold_in(arg_keys[10], 1), 0, INDEX_DEV - 1).astype(jnp.int32)
    pos_slot = with_ends(jax.random.randint(arg_keys[11], (QUERIES,), 0, P_DEV), jax.random.fold_in(arg_keys[11], 1), 0, P_DEV - 1).astype(jnp.int32)
    return {"passage_tokens": passage_tokens, "query_tokens": query_tokens, "norm_gain": norm_gain, "w_gate": w_gate, "w_up": w_up, "w_down": w_down, "old_head": old_head, "new_head": new_head, "stale_index": stale_index, "neg_owner": neg_owner, "neg_row": neg_row, "pos_slot": pos_slot}


TAU = 0.02

def encode(tokens, norm_gain, w_gate, w_up, w_down):
    gain = norm_gain.astype(jnp.float32)

    def one_sequence(sequence):
        values = sequence.astype(jnp.float32)
        scale = lax.rsqrt(lax.optimization_barrier(jnp.mean(values * values, axis=1, keepdims=True)) + 1e-06)
        normed = (values * scale * gain).astype(jnp.bfloat16)
        gate = jnp.dot(normed, w_gate, preferred_element_type=jnp.float32)
        up = jnp.dot(normed, w_up, preferred_element_type=jnp.float32)
        hidden = (jax.nn.gelu(gate, approximate=True) * up).astype(jnp.bfloat16)
        output = values + jnp.dot(hidden, w_down, preferred_element_type=jnp.float32)
        return lax.optimization_barrier(jnp.mean(output, axis=0))
    return lax.map(one_sequence, tokens).astype(jnp.bfloat16)

def reference(passage_tokens, query_tokens, norm_gain, w_gate, w_up, w_down, old_head, new_head, stale_index, neg_owner, neg_row, pos_slot):
    pooled_p = encode(passage_tokens, norm_gain, w_gate, w_up, w_down)
    pooled_q = encode(query_tokens, norm_gain, w_gate, w_up, w_down)
    refreshed = jnp.dot(pooled_p, old_head, preferred_element_type=jnp.float32).astype(jnp.bfloat16)
    query_emb = jnp.dot(pooled_q, new_head, preferred_element_type=jnp.float32)
    shard_of = jnp.arange(QUERIES, dtype=jnp.int32) // Q_DEV
    positive = jnp.take(refreshed, (shard_of * P_DEV + pos_slot).astype(jnp.int32), axis=0)
    row_ids = (neg_owner * INDEX_DEV + neg_row).astype(jnp.int32).reshape(-1)
    negative = jnp.take(stale_index, row_ids, axis=0).reshape(QUERIES, K, E)
    candidates = jnp.concatenate([positive[:, None, :], negative], axis=1).astype(jnp.float32)
    inner = jnp.einsum('qe,qje->qj', query_emb, candidates, precision=lax.Precision.HIGHEST)
    cand_norm = jnp.sqrt(lax.optimization_barrier(jnp.sum(candidates * candidates, axis=2)) + 1e-06)
    query_norm = jnp.sqrt(lax.optimization_barrier(jnp.sum(query_emb * query_emb, axis=1)) + 1e-06)
    scores = inner / (cand_norm * query_norm[:, None] * TAU)
    exps = jnp.exp(scores)
    exp_total = lax.optimization_barrier(jnp.sum(exps, axis=1))
    losses = jnp.log(exp_total) - scores[:, 0]
    first = (jnp.arange(K + 1) == 0).astype(jnp.float32)
    weights = (exps / exp_total[:, None] - first[None, :]) / QUERIES
    direct = jnp.einsum('qj,qje->qe', weights / (cand_norm * query_norm[:, None] * TAU), candidates, precision=lax.Precision.HIGHEST)
    radial = lax.optimization_barrier(jnp.sum(weights * scores, axis=1)) / (query_norm * query_norm)
    query_grad = direct - radial[:, None] * query_emb
    head_grad = jnp.dot(pooled_q.astype(jnp.float32).T, query_grad, precision=lax.Precision.HIGHEST)
    return (refreshed, losses, head_grad)
```

```python
import functools
import math

import jax
import jax.numpy as jnp
import numpy as np
from jax import lax
from jax.experimental import pallas as pl
from jax.experimental.pallas import tpu as pltpu
from jax.sharding import PartitionSpec as P

TAU = 0.02
MIB = 1024 * 1024


def params(mib=8):
    return pltpu.CompilerParams(vmem_limit_bytes=mib * MIB)


def in_hbm():
    return pl.BlockSpec(memory_space=pltpu.HBM)


def whole():
    return pl.BlockSpec(memory_space=pltpu.VMEM)


def gelu(v):
    c = math.sqrt(2.0 / math.pi)
    return 0.5 * v * (1.0 + jnp.tanh(c * (v + 0.044715 * (v * v * v))))


def mp_move(block, step, flip):
    n = lax.axis_size("mp") // 2
    perm = [(x * 2 + c, ((x + step) % n) * 2 + (c ^ flip)) for x in range(n) for c in range(2)]
    return lax.ppermute(block, "mp", perm)


def mate_move(block):
    return lax.ppermute(block, "section", [(s, s ^ 1) for s in range(lax.axis_size("section"))])


def half_move(block):
    sections, shards_n = lax.axis_size("section"), lax.axis_size("dp")
    turn = sections // 2 if (sections // 2) % 2 == 0 else 0
    perm = [
        (s * shards_n + d, ((s + turn) % sections) * shards_n + (d + shards_n // 2) % shards_n)
        for s in range(sections)
        for d in range(shards_n)
    ]
    return lax.ppermute(block, ("section", "dp"), perm)


def along_y(block):
    n = lax.axis_size("dp") // 2
    groups = [[h * n + y for y in range(n)] for h in range(2)]
    return lax.all_gather(block, "dp", axis=0, axis_index_groups=groups, tiled=True)


def x_ring(block, rows, wanted):
    low, high, wanted = lax.optimization_barrier((mp_move(block, 1, 0), mp_move(block, -1, 0), wanted))
    top, bottom = mp_move(low[:rows], 1, 0), mp_move(high[rows:], -1, 0)
    mine = jnp.concatenate([block, low, high, top, bottom], axis=0)
    return mine, mp_move(mine, 0, 1), wanted


def cut_kernel(gate_in, up_in, down_in, own, other, gate, up, down, sems):
    fetches = [
        pltpu.make_async_copy(source, target, sems.at[k])
        for k, (source, target) in enumerate(((gate_in, gate), (up_in, up), (down_in, down)))
    ]
    for fetch in fetches:
        fetch.start()
    units = gate.shape[1] // 2
    cut = units // 128 * 128
    gap = own.shape[1] - 3 * units
    own[:, 3 * units :] = jnp.zeros((own.shape[0], gap), own.dtype)
    other[:, :gap] = jnp.zeros((own.shape[0], gap), own.dtype)
    for fetch in fetches:
        fetch.wait()
    for half in range(2):

        @pl.when(lax.axis_index("section") % 2 == half)
        def _(first=half * units):
            turned = down[first : first + units, :].astype(jnp.float32).T.astype(jnp.bfloat16)
            own[:, 2 * units : 3 * units] = turned
            other[:, gap : gap + units] = turned
            for out, base in ((own, 0), (other, gap + units)):
                out[:, base : base + cut] = gate[:, first : first + cut]
                out[:, base + cut : base + units] = gate[:, first + cut : first + units]
                out[:, base + units : base + 2 * units - cut] = up[:, first + cut : first + units]
                out[:, base + 2 * units - cut : base + 2 * units] = up[:, first : first + cut]


def norm_kernel(nx, rows, near, far, out):
    step_rows = 32
    width = near.shape[1]
    x, c = lax.axis_index("mp") // 2, lax.axis_index("mp") % 2
    sides = []
    for ref, core in ((near, c), (far, 1 - c)):
        for k, step in enumerate((0, -1, 1, 2)):
            place = lax.rem(x + step + nx, nx) * 2 + core
            at = pl.ds(pl.multiple_of(place * width, width), width)
            sides.append((ref, k * (rows + 16), at))
    gains = [ref[first + rows : first + rows + 1, :].astype(jnp.float32) for ref, first, _ in sides]

    def body(i, carry):
        start = i * step_rows
        total = jnp.zeros((step_rows, width), jnp.float32)
        for ref, first, _ in sides:
            v = ref[pl.ds(pl.multiple_of(first + start, 16), step_rows), :].astype(jnp.float32)
            total = total + v * v
        scale = lax.rsqrt(jnp.sum(total, axis=1, keepdims=True) / (len(sides) * width) + 1e-06)
        target = pl.ds(pl.multiple_of(start, step_rows), step_rows)
        for (ref, first, at), gain in zip(sides, gains):
            v = ref[pl.ds(pl.multiple_of(first + start, 16), step_rows), :].astype(jnp.float32)
            out[target, at] = (v * scale * gain).astype(jnp.bfloat16)
        return carry

    lax.fori_loop(0, rows // step_rows, body, 0)


def marks(owner, shard_n):
    count = owner.shape[1]
    hit = lax.broadcasted_iota(jnp.int32, (shard_n, count), 0) == owner
    place = lax.broadcasted_iota(jnp.int32, (shard_n, count), 1).astype(jnp.float32)
    first = jnp.min(jnp.where(hit, place, 2.0 * count), axis=1, keepdims=True)
    last = jnp.max(jnp.where(hit, place, -1.0), axis=1, keepdims=True)
    return jnp.where(hit & (place == first), 1.0, 0.0), jnp.where(hit & (place == last) & (last > first), 1.0, 0.0)


def ask_kernel(owner, row, out):
    first, second = marks(owner[...], out.shape[0])
    wanted = row[...].astype(jnp.float32)
    one = jnp.sum(first * wanted, axis=1, keepdims=True)
    two = jnp.sum(second * wanted, axis=1, keepdims=True)
    lane = lax.broadcasted_iota(jnp.int32, out.shape, 1)
    out[...] = jnp.where(lane == 0, one, jnp.where(lane == 1, two, 0.0)).astype(jnp.int32)


def find_kernel(wanted, index, out):
    width, count = index.shape
    row = lax.broadcasted_iota(jnp.int32, (wanted.shape[0], count), 1)
    gap = jnp.zeros((wanted.shape[0], 128 - width), jnp.float32)
    for slot in range(2):
        hit = jnp.where(row == wanted[:, slot : slot + 1], 1.0, 0.0).astype(jnp.bfloat16)
        found = lax.dot_general(hit, index[...], (((1,), (1,)), ((), ())), preferred_element_type=jnp.float32)
        out[:, slot, :] = jnp.concatenate([found, gap], axis=1)


def hidden_kernel(units, normed, pool, weights, out, up_w, down_w, hidden, sems):
    h = lax.axis_index("dp") // (lax.axis_size("dp") // 2)
    rows = weights.shape[0]
    up_copies = [
        pltpu.make_async_copy(
            weights.at[:, pl.ds(4 * units * side, 2 * units)],
            up_w.at[pl.ds(pl.multiple_of((1 - h if side else h) * rows, rows), rows), :],
            sems.at[side],
        )
        for side in range(2)
    ]
    down_copy = pltpu.make_async_copy(weights.at[:, pl.ds(2 * units, 2 * units)], down_w, sems.at[2])
    for copy in up_copies + [down_copy]:
        copy.start()
    for copy in up_copies:
        copy.wait()
    cut = units // 128 * 128
    tail = units - cut
    both = jnp.dot(normed[...], up_w[...], preferred_element_type=jnp.float32)
    hidden[:, :cut] = (gelu(both[:, :cut]) * both[:, 2 * units - cut :]).astype(jnp.bfloat16)
    if tail:
        edge = both[:, cut : cut + 2 * tail]
        hidden[:, cut : cut + 2 * tail] = (gelu(edge) * pltpu.roll(edge, tail, 1)).astype(jnp.bfloat16)
    value = jnp.dot(pool[...], hidden[...], preferred_element_type=jnp.float32)[:, :units]
    high = value.astype(jnp.bfloat16).astype(jnp.float32)
    low = value - high
    both_parts = jnp.concatenate([high, low], axis=0)
    none = jnp.zeros_like(both_parts)
    own_rows = jnp.concatenate([both_parts, none], axis=1)
    other_rows = jnp.concatenate([none, both_parts], axis=1)
    sides = jnp.concatenate([own_rows, other_rows], axis=0).astype(jnp.bfloat16)
    down_copy.wait()
    total = lax.dot_general(sides, down_w[...], (((1,), (1,)), ((), ())), preferred_element_type=jnp.float32)
    mp_n, _, width = out.shape[0] // 2, out.shape[1], out.shape[2]
    for side in range(2):
        sums = total[side * 32 : side * 32 + 16] + total[side * 32 + 16 : side * 32 + 32]
        for mate in range(2):
            base = mate * mp_n + (1 - h if side else h) * (mp_n // 2)
            for k in range(mp_n // 2):
                out[base + k] = sums[mate * 8 : mate * 8 + 8, k * width : (k + 1) * width]


def head_kernel(p_count, lanes, parts, residual, old_head, new_head, owner, fetched, pooled_out, message, old, new, sems):
    fetches = [pltpu.make_async_copy(old_head, old, sems.at[0]), pltpu.make_async_copy(new_head, new, sems.at[1])]
    for fetch in fetches:
        fetch.start()
    total = residual[...]
    for k in range(parts.shape[0]):
        total = total + parts[k]
    pooled = total.astype(jnp.bfloat16)
    pooled_out[...] = pooled
    for fetch in fetches:
        fetch.wait()
    of_old = jnp.dot(pooled, old[...], preferred_element_type=jnp.float32)
    of_new = jnp.dot(pooled, new[...], preferred_element_type=jnp.float32)
    row = lax.broadcasted_iota(jnp.int32, of_old.shape, 0)
    term = jnp.where(row < p_count, of_old, of_new)
    gap = jnp.zeros((term.shape[0], 128 - lanes), jnp.float32)
    pieces = [
        jnp.concatenate([term[:, k * lanes : (k + 1) * lanes], gap], axis=1) for k in range(term.shape[1] // lanes)
    ]
    negatives = jnp.zeros((owner.shape[1], 128), jnp.float32)
    for slot, mark in enumerate(marks(owner[...], fetched.shape[0])):
        negatives = negatives + lax.dot_general(
            mark.astype(jnp.bfloat16),
            fetched[:, slot, :].astype(jnp.bfloat16),
            (((0,), (0,)), ((), ())),
            preferred_element_type=jnp.float32,
        )
    rows = jnp.concatenate(pieces + [negatives], axis=0).astype(jnp.bfloat16)
    for copy in range(message.shape[0]):
        message[copy] = rows


def loss_kernel(p_count, q_count, queries, slot, messages, pooled, fresh_out, loss_out, message, held):
    n = messages.shape[0]
    rows = messages[...].astype(jnp.float32)
    total = rows[0, : n * 8]
    for k in range(1, n):
        total = total + rows[k, : n * 8]
    emb = jnp.concatenate([total[a * 8 : (a + 1) * 8] for a in range(n)], axis=1)
    fresh = emb[:p_count].astype(jnp.bfloat16).astype(jnp.float32)
    held[:p_count] = fresh
    own = held[:, pl.ds(pl.multiple_of(lax.axis_index("mp") * 128, 128), 128)]
    fresh_out[...] = own[:p_count, : fresh_out.shape[1]].astype(jnp.bfloat16)
    k_count = (rows.shape[1] - n * 8) // q_count
    loss_rows, grad_rows = [], []
    for q in range(q_count):
        query = emb[p_count + q : p_count + q + 1]
        positive = fresh[0:1]
        for k in range(1, p_count):
            positive = jnp.where(slot[q] == k, fresh[k : k + 1], positive)
        tiles = [rows[a, n * 8 + q * k_count : n * 8 + (q + 1) * k_count] for a in range(n)]
        inner = jnp.zeros((k_count, 128), jnp.float32)
        square = inner
        for a in range(n):
            inner = inner + tiles[a] * query[:, a * 128 : (a + 1) * 128]
            square = square + tiles[a] * tiles[a]
        inner = jnp.sum(inner, axis=1, keepdims=True)
        square = jnp.sum(square, axis=1, keepdims=True)
        query_norm = jnp.sqrt(jnp.sum(query * query, axis=1, keepdims=True) + 1e-06)
        below = jnp.sqrt(square + 1e-06) * query_norm * TAU
        scores = inner / below
        below_p = jnp.sqrt(jnp.sum(positive * positive, axis=1, keepdims=True) + 1e-06) * query_norm * TAU
        score_p = jnp.sum(positive * query, axis=1, keepdims=True) / below_p
        exps, exp_p = jnp.exp(scores), jnp.exp(score_p)
        total = jnp.sum(exps, axis=0, keepdims=True) + exp_p
        loss_rows.append(jnp.log(total) - score_p)
        weights = exps / total / queries
        weight_p = (exp_p / total - 1.0) / queries
        radial = (jnp.sum(weights * scores, axis=0, keepdims=True) + weight_p * score_p) / (query_norm * query_norm)
        share = weights / below
        direct = jnp.concatenate([jnp.sum(share * tile, axis=0, keepdims=True) for tile in tiles], axis=1)
        grad_rows.append(direct + (weight_p / below_p) * positive - radial * query)
    losses = jnp.concatenate(loss_rows, axis=0)
    loss_out[...] = jnp.broadcast_to(losses, loss_out.shape)
    grads = jnp.concatenate(grad_rows, axis=0).astype(jnp.bfloat16)
    width = pooled.shape[1]
    features = pooled[...].astype(jnp.float32)[p_count : p_count + q_count].astype(jnp.bfloat16)
    columns = lax.axis_size("dp")
    for k in range(message.shape[0]):
        at = k % columns * n // columns * 128
        message[k, :, :width] = features
        message[k, :, width:] = grads[:, at : at + 128]


def grad_kernel(width, arrived, out):
    block = out.shape[0]
    both = lax.dot_general(
        arrived[:, width:], arrived[:, :width], (((0,), (0,)), ((), ())), preferred_element_type=jnp.float32
    )
    shared = lax.axis_size("dp") // lax.axis_size("mp")
    chosen = both[:block]
    for k in range(1, shared):
        chosen = jnp.where(lax.axis_index("dp") % shared == k, both[k * block : (k + 1) * block], chosen)
    out[...] = chosen


def shards(
    passage_tokens,
    query_tokens,
    norm_gain,
    w_gate,
    w_up,
    w_down,
    old_head,
    new_head,
    stale_index,
    neg_owner,
    neg_row,
    pos_slot,
):
    p_count, length, width = passage_tokens.shape
    q_count, q_length, _ = query_tokens.shape
    k_count = neg_owner.shape[1]
    embed = old_head.shape[1]
    sections = lax.axis_size("section")
    shard_count = sections * lax.axis_size("dp")
    mp_n = lax.axis_size("mp")
    features = width * mp_n
    f32, bf16 = jnp.float32, jnp.bfloat16

    units = w_gate.shape[1] // 2
    cut = units // 128 * 128
    wide = -(-3 * units // 128) * 128
    own, other = pl.pallas_call(
        cut_kernel,
        out_shape=[jax.ShapeDtypeStruct((w_gate.shape[0], wide), bf16)] * 2,
        in_specs=[in_hbm()] * 3,
        out_specs=[whole()] * 2,
        scratch_shapes=[pltpu.VMEM(w.shape, bf16) for w in (w_gate, w_up, w_down)] + [pltpu.SemaphoreType.DMA((3,))],
        compiler_params=params(56),
        name="cut",
    )(w_gate, w_up, w_down)
    other = half_move(other)

    rows = p_count * length + q_count * q_length
    gain_rows = jnp.broadcast_to(norm_gain[None, :], (16, width))
    tokens = jnp.concatenate([passage_tokens.reshape(-1, width), query_tokens.reshape(-1, width)], axis=0)
    other, mate_tokens = lax.optimization_barrier((other, mate_move(tokens)))

    edge = wide - 128
    merged = jnp.concatenate([own[:, :edge], own[:, edge:] + other[:, :128], other[:, 128:]], axis=1)
    weights = along_y(merged)

    flip = lax.axis_index("section") % 2 == 1
    tokens = jnp.concatenate(
        [jnp.where(flip, mate_tokens, tokens), jnp.where(flip, tokens, mate_tokens), gain_rows], axis=0
    )
    request_count = q_count * k_count
    owner = neg_owner.reshape(1, request_count)
    requests = pl.pallas_call(
        ask_kernel,
        out_shape=jax.ShapeDtypeStruct((shard_count, 128), jnp.int32),
        in_specs=[whole()] * 2,
        out_specs=whole(),
        compiler_params=params(),
        name="ask",
    )(owner, neg_row.reshape(1, request_count))
    wanted = lax.all_to_all(requests, ("section", "dp"), 0, 0, tiled=True)
    near, far, wanted = x_ring(tokens, rows, wanted)
    found = pl.pallas_call(
        find_kernel,
        out_shape=jax.ShapeDtypeStruct((shard_count, 2, 128), f32),
        in_specs=[whole()] * 2,
        out_specs=whole(),
        compiler_params=params(),
        name="find",
    )(wanted, stale_index.T)
    fetched = lax.all_to_all(found, ("section", "dp"), 0, 0, tiled=True)

    normed = pl.pallas_call(
        functools.partial(norm_kernel, mp_n // 2, 2 * rows),
        out_shape=jax.ShapeDtypeStruct((2 * rows, features), bf16),
        in_specs=[whole()] * 2,
        out_specs=whole(),
        compiler_params=params(16),
        name="norm",
    )(near, far)

    pool = np.zeros((16, 2 * rows), np.float32)
    for mate in range(2):
        base = mate * rows
        for k in range(p_count):
            pool[mate * 8 + k, base + k * length : base + (k + 1) * length] = 1.0 / length
        base += p_count * length
        for k in range(q_count):
            pool[mate * 8 + p_count + k, base + k * q_length : base + (k + 1) * q_length] = 1.0 / q_length
    padded = cut + 2 * (units - cut)
    parts = pl.pallas_call(
        functools.partial(hidden_kernel, units),
        out_shape=jax.ShapeDtypeStruct((2 * mp_n, 8, width), f32),
        in_specs=[whole(), whole(), in_hbm()],
        out_specs=whole(),
        scratch_shapes=[
            pltpu.VMEM((features, 2 * units), bf16),
            pltpu.VMEM((features // 2, 2 * units), bf16),
            pltpu.VMEM((2 * rows, padded), bf16),
            pltpu.SemaphoreType.DMA((3,)),
        ],
        compiler_params=params(52),
        name="hidden",
    )(normed, jnp.asarray(pool, bf16), weights)

    groups = [[s * mp_n + m for s in (p, p + 1) for m in range(mp_n)] for p in range(0, sections, 2)]
    parts = lax.all_to_all(
        parts, ("section", "mp"), split_axis=0, concat_axis=0, axis_index_groups=groups, tiled=True
    )
    residual = jnp.concatenate(
        [
            jnp.sum(passage_tokens.astype(f32), axis=1) / length,
            jnp.sum(query_tokens.astype(f32), axis=1) / q_length,
            jnp.zeros((8 - p_count - q_count, width), f32),
        ],
        axis=0,
    )
    own_width = embed // mp_n
    message_rows = 8 * mp_n + request_count
    pooled, message = pl.pallas_call(
        functools.partial(head_kernel, p_count, own_width),
        out_shape=[
            jax.ShapeDtypeStruct((8, width), bf16),
            jax.ShapeDtypeStruct((mp_n, message_rows, 128), bf16),
        ],
        in_specs=[whole()] * 2 + [in_hbm()] * 2 + [whole()] * 2,
        out_specs=[whole()] * 2,
        scratch_shapes=[
            pltpu.VMEM((width, embed), bf16),
            pltpu.VMEM((width, embed), bf16),
            pltpu.SemaphoreType.DMA((2,)),
        ],
        compiler_params=params(),
        name="head",
    )(parts, residual, old_head, new_head, owner, fetched)
    messages = lax.all_to_all(message, "mp", 0, 0, tiled=True)

    refreshed, losses, message = pl.pallas_call(
        functools.partial(loss_kernel, p_count, q_count, q_count * shard_count),
        out_shape=[
            jax.ShapeDtypeStruct((p_count, own_width), bf16),
            jax.ShapeDtypeStruct((q_count, 128), f32),
            jax.ShapeDtypeStruct((shard_count, q_count, width + 128), bf16),
        ],
        in_specs=[pl.BlockSpec(memory_space=pltpu.SMEM)] + [whole()] * 2,
        out_specs=[whole()] * 3,
        scratch_shapes=[pltpu.VMEM((8, 128 * mp_n), f32)],
        compiler_params=params(),
        name="loss",
    )(pos_slot, messages, pooled)

    arrived = lax.all_to_all(message, ("section", "dp"), 0, 0, tiled=True)
    head_grad = pl.pallas_call(
        functools.partial(grad_kernel, width),
        out_shape=jax.ShapeDtypeStruct((embed // lax.axis_size("dp"), width), f32),
        in_specs=[whole()],
        out_specs=whole(),
        compiler_params=params(),
        name="grad",
    )(arrived.reshape(-1, width + 128)).T
    return (refreshed, losses[:, 0], head_grad)


def solution(mesh):
    placed = (
        P(("section", "dp"), None, "mp"),
        P(("section", "dp"), None, "mp"),
        P("mp"),
        P("dp", "mp"),
        P("dp", "mp"),
        P("mp", "dp"),
        P("mp", None),
        P("mp", None),
        P(("section", "dp"), "mp"),
        P(("section", "dp"), None),
        P(("section", "dp"), None),
        P(("section", "dp")),
    )
    return jax.shard_map(
        shards,
        mesh=mesh,
        in_specs=placed,
        out_specs=(P(("section", "dp"), "mp"), P(("section", "dp")), P("mp", "dp")),
        check_vma=False,
    )
```

```python
import functools
import math

import jax
import jax.numpy as jnp
import numpy as np
from jax import lax
from jax.experimental import pallas as pl
from jax.experimental.pallas import tpu as pltpu
from jax.sharding import PartitionSpec as P

TAU = 0.02
MIB = 1024 * 1024


def params(mib=8):
    return pltpu.CompilerParams(vmem_limit_bytes=mib * MIB)


def in_hbm():
    return pl.BlockSpec(memory_space=pltpu.HBM)


def whole():
    return pl.BlockSpec(memory_space=pltpu.VMEM)


def gelu(v):
    c = math.sqrt(2.0 / math.pi)
    return 0.5 * v * (1.0 + jnp.tanh(c * (v + 0.044715 * (v * v * v))))


def mp_move(block, step, flip):
    n = lax.axis_size("mp") // 2
    perm = [(x * 2 + c, ((x + step) % n) * 2 + (c ^ flip)) for x in range(n) for c in range(2)]
    return lax.ppermute(block, "mp", perm)


def mate_move(block):
    return lax.ppermute(block, "section", [(s, s ^ 1) for s in range(lax.axis_size("section"))])


def half_move(block):
    sections, shards_n = lax.axis_size("section"), lax.axis_size("dp")
    turn = sections // 2 if (sections // 2) % 2 == 0 else 0
    perm = [
        (s * shards_n + d, ((s + turn) % sections) * shards_n + (d + shards_n // 2) % shards_n)
        for s in range(sections)
        for d in range(shards_n)
    ]
    return lax.ppermute(block, ("section", "dp"), perm)


def along_y(block):
    n = lax.axis_size("dp") // 2
    groups = [[h * n + y for y in range(n)] for h in range(2)]
    return lax.all_gather(block, "dp", axis=0, axis_index_groups=groups, tiled=True)


def x_blocks(block, wanted):
    others = [mp_move(block, step, 0) for step in (1, -1, 2)]
    others, wanted = lax.optimization_barrier((others, wanted))
    mine = jnp.concatenate([block] + others, axis=0)
    return mine, mp_move(mine, 0, 1), wanted


def cut_kernel(gate_in, up_in, down_in, own, other, gate, up, down, sems):
    fetches = [
        pltpu.make_async_copy(source, target, sems.at[k])
        for k, (source, target) in enumerate(((gate_in, gate), (up_in, up), (down_in, down)))
    ]
    for fetch in fetches:
        fetch.start()
    units = gate.shape[1] // 2
    cut = units // 128 * 128
    gap = own.shape[1] - 3 * units
    own[:, 3 * units :] = jnp.zeros((own.shape[0], gap), own.dtype)
    other[:, :gap] = jnp.zeros((own.shape[0], gap), own.dtype)
    for fetch in fetches:
        fetch.wait()
    for half in range(2):

        @pl.when(lax.axis_index("section") % 2 == half)
        def _(first=half * units):
            turned = down[first : first + units, :].astype(jnp.float32).T.astype(jnp.bfloat16)
            own[:, 2 * units : 3 * units] = turned
            other[:, gap : gap + units] = turned
            for out, base in ((own, 0), (other, gap + units)):
                out[:, base : base + cut] = gate[:, first : first + cut]
                out[:, base + cut : base + units] = gate[:, first + cut : first + units]
                out[:, base + units : base + 2 * units - cut] = up[:, first + cut : first + units]
                out[:, base + 2 * units - cut : base + 2 * units] = up[:, first : first + cut]


def merge_kernel(own, other, out):
    edge = own.shape[1] - 128
    out[:, :edge] = own[:, :edge]
    out[:, edge : edge + 128] = own[:, edge:] + other[:, :128]
    out[:, edge + 128 :] = other[:, 128:]


def norm_kernel(nx, rows, near, far, out):
    step_rows = 32
    width = near.shape[1]
    x, c = lax.axis_index("mp") // 2, lax.axis_index("mp") % 2
    sides = []
    for ref, core in ((near, c), (far, 1 - c)):
        for k, step in enumerate((0, -1, 1, 2)):
            place = lax.rem(x + step + nx, nx) * 2 + core
            at = pl.ds(pl.multiple_of(place * width, width), width)
            sides.append((ref, k * (rows + 16), at))
    gains = [ref[first + rows : first + rows + 1, :].astype(jnp.float32) for ref, first, _ in sides]

    def body(i, carry):
        start = i * step_rows
        total = jnp.zeros((step_rows, width), jnp.float32)
        for ref, first, _ in sides:
            v = ref[pl.ds(pl.multiple_of(first + start, 16), step_rows), :].astype(jnp.float32)
            total = total + v * v
        scale = lax.rsqrt(jnp.sum(total, axis=1, keepdims=True) / (len(sides) * width) + 1e-06)
        target = pl.ds(pl.multiple_of(start, step_rows), step_rows)
        for (ref, first, at), gain in zip(sides, gains):
            v = ref[pl.ds(pl.multiple_of(first + start, 16), step_rows), :].astype(jnp.float32)
            out[target, at] = (v * scale * gain).astype(jnp.bfloat16)
        return carry

    lax.fori_loop(0, rows // step_rows, body, 0)


def marks(owner, shard_n):
    count = owner.shape[1]
    hit = lax.broadcasted_iota(jnp.int32, (shard_n, count), 0) == owner
    place = lax.broadcasted_iota(jnp.int32, (shard_n, count), 1).astype(jnp.float32)
    first = jnp.min(jnp.where(hit, place, 2.0 * count), axis=1, keepdims=True)
    last = jnp.max(jnp.where(hit, place, -1.0), axis=1, keepdims=True)
    return jnp.where(hit & (place == first), 1.0, 0.0), jnp.where(hit & (place == last) & (last > first), 1.0, 0.0)


def ask_kernel(owner, row, out):
    first, second = marks(owner[...], out.shape[0])
    wanted = row[...].astype(jnp.float32)
    one = jnp.sum(first * wanted, axis=1, keepdims=True)
    two = jnp.sum(second * wanted, axis=1, keepdims=True)
    lane = lax.broadcasted_iota(jnp.int32, out.shape, 1)
    out[...] = jnp.where(lane == 0, one, jnp.where(lane == 1, two, 0.0)).astype(jnp.int32)


def find_kernel(wanted, index, out):
    width, count = index.shape
    row = lax.broadcasted_iota(jnp.int32, (wanted.shape[0], count), 1)
    gap = jnp.zeros((wanted.shape[0], 128 - width), jnp.float32)
    for slot in range(2):
        hit = jnp.where(row == wanted[:, slot : slot + 1], 1.0, 0.0).astype(jnp.bfloat16)
        found = lax.dot_general(hit, index[...], (((1,), (1,)), ((), ())), preferred_element_type=jnp.float32)
        out[:, slot, :] = jnp.concatenate([found, gap], axis=1)


def hidden_kernel(units, normed, pool, weights, out, up_w, down_w, hidden, sems):
    h = lax.axis_index("dp") // (lax.axis_size("dp") // 2)
    rows = weights.shape[0]
    parts = 4
    piece = rows // parts
    copies = []
    for side, target in ((0, up_w), (2, up_w), (1, down_w)):
        base = rows if side == 2 else 0
        copies.append(
            [
                pltpu.make_async_copy(
                    weights.at[pl.ds(k * piece, piece), pl.ds(2 * units * side, 2 * units)],
                    target.at[pl.ds(base + k * piece, piece), :],
                    sems.at[side * parts + k],
                )
                for k in range(parts)
            ]
        )
    for group in copies:
        for copy in group:
            copy.start()
    both = None
    for side in range(2):
        for copy in copies[side]:
            copy.wait()
        columns = pl.ds(pl.multiple_of((1 - h if side else h) * rows, rows), rows)
        term = jnp.dot(
            normed[:, columns], up_w[side * rows : (side + 1) * rows, :], preferred_element_type=jnp.float32
        )
        both = term if both is None else both + term
    cut = units // 128 * 128
    tail = units - cut
    hidden[:, :cut] = (gelu(both[:, :cut]) * both[:, 2 * units - cut :]).astype(jnp.bfloat16)
    if tail:
        edge = both[:, cut : cut + 2 * tail]
        hidden[:, cut : cut + 2 * tail] = (gelu(edge) * pltpu.roll(edge, tail, 1)).astype(jnp.bfloat16)
    value = jnp.dot(pool[...], hidden[...], preferred_element_type=jnp.float32)[:, :units]
    high = value.astype(jnp.bfloat16).astype(jnp.float32)
    low = value - high
    both_parts = jnp.concatenate([high, low], axis=0)
    none = jnp.zeros_like(both_parts)
    own_rows = jnp.concatenate([both_parts, none], axis=1)
    other_rows = jnp.concatenate([none, both_parts], axis=1)
    sides = jnp.concatenate([own_rows, other_rows], axis=0).astype(jnp.bfloat16)
    for copy in copies[2]:
        copy.wait()
    total = lax.dot_general(sides, down_w[...], (((1,), (1,)), ((), ())), preferred_element_type=jnp.float32)
    mp_n, _, width = out.shape[0] // 2, out.shape[1], out.shape[2]
    for side in range(2):
        sums = total[side * 32 : side * 32 + 16] + total[side * 32 + 16 : side * 32 + 32]
        for mate in range(2):
            base = mate * mp_n + (1 - h if side else h) * (mp_n // 2)
            for k in range(mp_n // 2):
                out[base + k] = sums[mate * 8 : mate * 8 + 8, k * width : (k + 1) * width]


def head_kernel(p_count, lanes, parts, residual, old_head, new_head, owner, fetched, pooled_out, message, old, new, sems):
    fetches = [pltpu.make_async_copy(old_head, old, sems.at[0]), pltpu.make_async_copy(new_head, new, sems.at[1])]
    for fetch in fetches:
        fetch.start()
    total = residual[...]
    for k in range(parts.shape[0]):
        total = total + parts[k]
    pooled = total.astype(jnp.bfloat16)
    pooled_out[...] = pooled
    for fetch in fetches:
        fetch.wait()
    of_old = jnp.dot(pooled, old[...], preferred_element_type=jnp.float32)
    of_new = jnp.dot(pooled, new[...], preferred_element_type=jnp.float32)
    row = lax.broadcasted_iota(jnp.int32, of_old.shape, 0)
    term = jnp.where(row < p_count, of_old, of_new)
    gap = jnp.zeros((term.shape[0], 128 - lanes), jnp.float32)
    pieces = [
        jnp.concatenate([term[:, k * lanes : (k + 1) * lanes], gap], axis=1) for k in range(term.shape[1] // lanes)
    ]
    negatives = jnp.zeros((owner.shape[1], 128), jnp.float32)
    for slot, mark in enumerate(marks(owner[...], fetched.shape[0])):
        negatives = negatives + lax.dot_general(
            mark.astype(jnp.bfloat16),
            fetched[:, slot, :].astype(jnp.bfloat16),
            (((0,), (0,)), ((), ())),
            preferred_element_type=jnp.float32,
        )
    rows = jnp.concatenate(pieces + [negatives], axis=0).astype(jnp.bfloat16)
    for copy in range(message.shape[0]):
        message[copy] = rows


def loss_kernel(p_count, q_count, queries, slot, messages, pooled, fresh_out, loss_out, message, held):
    n = messages.shape[0]
    rows = messages[...].astype(jnp.float32)
    total = rows[0, : n * 8]
    for k in range(1, n):
        total = total + rows[k, : n * 8]
    emb = jnp.concatenate([total[a * 8 : (a + 1) * 8] for a in range(n)], axis=1)
    fresh = emb[:p_count].astype(jnp.bfloat16).astype(jnp.float32)
    held[:p_count] = fresh
    own = held[:, pl.ds(pl.multiple_of(lax.axis_index("mp") * 128, 128), 128)]
    fresh_out[...] = own[:p_count, : fresh_out.shape[1]].astype(jnp.bfloat16)
    k_count = (rows.shape[1] - n * 8) // q_count
    loss_rows, grad_rows = [], []
    for q in range(q_count):
        query = emb[p_count + q : p_count + q + 1]
        positive = fresh[0:1]
        for k in range(1, p_count):
            positive = jnp.where(slot[q] == k, fresh[k : k + 1], positive)
        tiles = [rows[a, n * 8 + q * k_count : n * 8 + (q + 1) * k_count] for a in range(n)]
        inner = jnp.zeros((k_count, 128), jnp.float32)
        square = inner
        for a in range(n):
            inner = inner + tiles[a] * query[:, a * 128 : (a + 1) * 128]
            square = square + tiles[a] * tiles[a]
        inner = jnp.sum(inner, axis=1, keepdims=True)
        square = jnp.sum(square, axis=1, keepdims=True)
        query_norm = jnp.sqrt(jnp.sum(query * query, axis=1, keepdims=True) + 1e-06)
        below = jnp.sqrt(square + 1e-06) * query_norm * TAU
        scores = inner / below
        below_p = jnp.sqrt(jnp.sum(positive * positive, axis=1, keepdims=True) + 1e-06) * query_norm * TAU
        score_p = jnp.sum(positive * query, axis=1, keepdims=True) / below_p
        exps, exp_p = jnp.exp(scores), jnp.exp(score_p)
        total = jnp.sum(exps, axis=0, keepdims=True) + exp_p
        loss_rows.append(jnp.log(total) - score_p)
        weights = exps / total / queries
        weight_p = (exp_p / total - 1.0) / queries
        radial = (jnp.sum(weights * scores, axis=0, keepdims=True) + weight_p * score_p) / (query_norm * query_norm)
        share = weights / below
        direct = jnp.concatenate([jnp.sum(share * tile, axis=0, keepdims=True) for tile in tiles], axis=1)
        grad_rows.append(direct + (weight_p / below_p) * positive - radial * query)
    losses = jnp.concatenate(loss_rows, axis=0)
    loss_out[...] = jnp.broadcast_to(losses, loss_out.shape)
    grads = jnp.concatenate(grad_rows, axis=0).astype(jnp.bfloat16)
    width = pooled.shape[1]
    features = pooled[...].astype(jnp.float32)[p_count : p_count + q_count].astype(jnp.bfloat16)
    columns = lax.axis_size("dp")
    for k in range(message.shape[0]):
        at = k % columns * n // columns * 128
        message[k, :, :width] = features
        message[k, :, width:] = grads[:, at : at + 128]


def grad_kernel(width, arrived, out):
    block = out.shape[0]
    both = lax.dot_general(
        arrived[:, width:], arrived[:, :width], (((0,), (0,)), ((), ())), preferred_element_type=jnp.float32
    )
    shared = lax.axis_size("dp") // lax.axis_size("mp")
    chosen = both[:block]
    for k in range(1, shared):
        chosen = jnp.where(lax.axis_index("dp") % shared == k, both[k * block : (k + 1) * block], chosen)
    out[...] = chosen


def shards(
    passage_tokens,
    query_tokens,
    norm_gain,
    w_gate,
    w_up,
    w_down,
    old_head,
    new_head,
    stale_index,
    neg_owner,
    neg_row,
    pos_slot,
):
    p_count, length, width = passage_tokens.shape
    q_count, q_length, _ = query_tokens.shape
    k_count = neg_owner.shape[1]
    embed = old_head.shape[1]
    sections = lax.axis_size("section")
    shard_count = sections * lax.axis_size("dp")
    mp_n = lax.axis_size("mp")
    features = width * mp_n
    f32, bf16 = jnp.float32, jnp.bfloat16

    units = w_gate.shape[1] // 2
    cut = units // 128 * 128
    wide = -(-3 * units // 128) * 128
    own, other = pl.pallas_call(
        cut_kernel,
        out_shape=[jax.ShapeDtypeStruct((w_gate.shape[0], wide), bf16)] * 2,
        in_specs=[in_hbm()] * 3,
        out_specs=[whole()] * 2,
        scratch_shapes=[pltpu.VMEM(w.shape, bf16) for w in (w_gate, w_up, w_down)] + [pltpu.SemaphoreType.DMA((3,))],
        compiler_params=params(56),
        name="cut",
    )(w_gate, w_up, w_down)
    other = half_move(other)

    rows = p_count * length + q_count * q_length
    gain_rows = jnp.broadcast_to(norm_gain[None, :], (16, width))
    tokens = jnp.concatenate([passage_tokens.reshape(-1, width), query_tokens.reshape(-1, width)], axis=0)
    request_count = q_count * k_count
    owner = neg_owner.reshape(1, request_count)
    requests = pl.pallas_call(
        ask_kernel,
        out_shape=jax.ShapeDtypeStruct((shard_count, 128), jnp.int32),
        in_specs=[whole()] * 2,
        out_specs=whole(),
        compiler_params=params(),
        name="ask",
    )(owner, neg_row.reshape(1, request_count))

    other, mate_tokens, requests = lax.optimization_barrier((other, mate_move(tokens), requests))
    merged = pl.pallas_call(
        merge_kernel,
        out_shape=jax.ShapeDtypeStruct((w_gate.shape[0], 6 * units), bf16),
        in_specs=[whole()] * 2,
        out_specs=whole(),
        compiler_params=params(),
        name="merge",
    )(own, other)
    weights = along_y(merged)

    flip = lax.axis_index("section") % 2 == 1
    tokens = jnp.concatenate(
        [jnp.where(flip, mate_tokens, tokens), jnp.where(flip, tokens, mate_tokens), gain_rows], axis=0
    )
    wanted = lax.all_to_all(requests, ("section", "dp"), 0, 0, tiled=True)
    near, far, wanted = x_blocks(tokens, wanted)
    found = pl.pallas_call(
        find_kernel,
        out_shape=jax.ShapeDtypeStruct((shard_count, 2, 128), f32),
        in_specs=[whole()] * 2,
        out_specs=whole(),
        compiler_params=params(),
        name="find",
    )(wanted, stale_index.T)
    fetched = lax.all_to_all(found, ("section", "dp"), 0, 0, tiled=True)

    normed = pl.pallas_call(
        functools.partial(norm_kernel, mp_n // 2, 2 * rows),
        out_shape=jax.ShapeDtypeStruct((2 * rows, features), bf16),
        in_specs=[whole()] * 2,
        out_specs=whole(),
        compiler_params=params(16),
        name="norm",
    )(near, far)

    pool = np.zeros((16, 2 * rows), np.float32)
    for mate in range(2):
        base = mate * rows
        for k in range(p_count):
            pool[mate * 8 + k, base + k * length : base + (k + 1) * length] = 1.0 / length
        base += p_count * length
        for k in range(q_count):
            pool[mate * 8 + p_count + k, base + k * q_length : base + (k + 1) * q_length] = 1.0 / q_length
    padded = cut + 2 * (units - cut)
    parts = pl.pallas_call(
        functools.partial(hidden_kernel, units),
        out_shape=jax.ShapeDtypeStruct((2 * mp_n, 8, width), f32),
        in_specs=[whole(), whole(), in_hbm()],
        out_specs=whole(),
        scratch_shapes=[
            pltpu.VMEM((features, 2 * units), bf16),
            pltpu.VMEM((features // 2, 2 * units), bf16),
            pltpu.VMEM((2 * rows, padded), bf16),
            pltpu.SemaphoreType.DMA((12,)),
        ],
        compiler_params=params(52),
        name="hidden",
    )(normed, jnp.asarray(pool, bf16), weights)

    groups = [[s * mp_n + m for s in (p, p + 1) for m in range(mp_n)] for p in range(0, sections, 2)]
    parts = lax.all_to_all(
        parts, ("section", "mp"), split_axis=0, concat_axis=0, axis_index_groups=groups, tiled=True
    )
    residual = jnp.concatenate(
        [
            jnp.sum(passage_tokens.astype(f32), axis=1) / length,
            jnp.sum(query_tokens.astype(f32), axis=1) / q_length,
            jnp.zeros((8 - p_count - q_count, width), f32),
        ],
        axis=0,
    )
    own_width = embed // mp_n
    message_rows = 8 * mp_n + request_count
    pooled, message = pl.pallas_call(
        functools.partial(head_kernel, p_count, own_width),
        out_shape=[
            jax.ShapeDtypeStruct((8, width), bf16),
            jax.ShapeDtypeStruct((mp_n, message_rows, 128), bf16),
        ],
        in_specs=[whole()] * 2 + [in_hbm()] * 2 + [whole()] * 2,
        out_specs=[whole()] * 2,
        scratch_shapes=[
            pltpu.VMEM((width, embed), bf16),
            pltpu.VMEM((width, embed), bf16),
            pltpu.SemaphoreType.DMA((2,)),
        ],
        compiler_params=params(),
        name="head",
    )(parts, residual, old_head, new_head, owner, fetched)
    messages = lax.all_to_all(message, "mp", 0, 0, tiled=True)

    refreshed, losses, message = pl.pallas_call(
        functools.partial(loss_kernel, p_count, q_count, q_count * shard_count),
        out_shape=[
            jax.ShapeDtypeStruct((p_count, own_width), bf16),
            jax.ShapeDtypeStruct((q_count, 128), f32),
            jax.ShapeDtypeStruct((shard_count, q_count, width + 128), bf16),
        ],
        in_specs=[pl.BlockSpec(memory_space=pltpu.SMEM)] + [whole()] * 2,
        out_specs=[whole()] * 3,
        scratch_shapes=[pltpu.VMEM((8, 128 * mp_n), f32)],
        compiler_params=params(),
        name="loss",
    )(pos_slot, messages, pooled)

    arrived = lax.all_to_all(message, ("section", "dp"), 0, 0, tiled=True)
    head_grad = pl.pallas_call(
        functools.partial(grad_kernel, width),
        out_shape=jax.ShapeDtypeStruct((embed // lax.axis_size("dp"), width), f32),
        in_specs=[whole()],
        out_specs=whole(),
        compiler_params=params(),
        name="grad",
    )(arrived.reshape(-1, width + 128)).T
    return (refreshed, losses[:, 0], head_grad)


def solution(mesh):
    placed = (
        P(("section", "dp"), None, "mp"),
        P(("section", "dp"), None, "mp"),
        P("mp"),
        P("dp", "mp"),
        P("dp", "mp"),
        P("mp", "dp"),
        P("mp", None),
        P("mp", None),
        P(("section", "dp"), "mp"),
        P(("section", "dp"), None),
        P(("section", "dp"), None),
        P(("section", "dp")),
    )
    return jax.shard_map(
        shards,
        mesh=mesh,
        in_specs=placed,
        out_specs=(P(("section", "dp"), "mp"), P(("section", "dp")), P("mp", "dp")),
        check_vma=False,
    )
```

```python
import functools
import math

import jax
import jax.numpy as jnp
import numpy as np
from jax import lax
from jax.experimental import pallas as pl
from jax.experimental.pallas import tpu as pltpu
from jax.sharding import PartitionSpec as P

TAU = 0.02
MIB = 1024 * 1024


def params(mib=8):
    return pltpu.CompilerParams(vmem_limit_bytes=mib * MIB)


def in_hbm():
    return pl.BlockSpec(memory_space=pltpu.HBM)


def whole():
    return pl.BlockSpec(memory_space=pltpu.VMEM)


def gelu(v):
    c = math.sqrt(2.0 / math.pi)
    return 0.5 * v * (1.0 + jnp.tanh(c * (v + 0.044715 * (v * v * v))))


def mp_move(block, step, flip):
    n = lax.axis_size("mp") // 2
    perm = [(x * 2 + c, ((x + step) % n) * 2 + (c ^ flip)) for x in range(n) for c in range(2)]
    return lax.ppermute(block, "mp", perm)


def mate_move(block):
    return lax.ppermute(block, "section", [(s, s ^ 1) for s in range(lax.axis_size("section"))])


def half_move(block):
    sections, shards_n = lax.axis_size("section"), lax.axis_size("dp")
    turn = sections // 2 if (sections // 2) % 2 == 0 else 0
    perm = [
        (s * shards_n + d, ((s + turn) % sections) * shards_n + (d + shards_n // 2) % shards_n)
        for s in range(sections)
        for d in range(shards_n)
    ]
    return lax.ppermute(block, ("section", "dp"), perm)


def along_y(block):
    n = lax.axis_size("dp") // 2
    groups = [[h * n + y for y in range(n)] for h in range(2)]
    return lax.all_gather(block, "dp", axis=0, axis_index_groups=groups, tiled=True)


def spread(block, low, high, wanted):
    mine = jnp.concatenate([block, low, high, mp_move(block, 2, 0)], axis=0)
    mate, wanted = lax.optimization_barrier((mate_move(mine), wanted))
    mine = jnp.concatenate([mine, mate], axis=0)
    return mine, mp_move(mine, 0, 1), wanted


def cut_kernel(gate_in, up_in, down_in, own, other, gate, up, down, sems):
    fetches = [
        pltpu.make_async_copy(source, target, sems.at[k])
        for k, (source, target) in enumerate(((gate_in, gate), (up_in, up), (down_in, down)))
    ]
    for fetch in fetches:
        fetch.start()
    units = gate.shape[1] // 2
    cut = units // 128 * 128
    gap = own.shape[1] - 3 * units
    own[:, 3 * units :] = jnp.zeros((own.shape[0], gap), own.dtype)
    other[:, :gap] = jnp.zeros((own.shape[0], gap), own.dtype)
    for fetch in fetches:
        fetch.wait()
    for half in range(2):

        @pl.when(lax.axis_index("section") % 2 == half)
        def _(first=half * units):
            turned = down[first : first + units, :].astype(jnp.float32).T.astype(jnp.bfloat16)
            own[:, 2 * units : 3 * units] = turned
            other[:, gap : gap + units] = turned
            for out, base in ((own, 0), (other, gap + units)):
                out[:, base : base + cut] = gate[:, first : first + cut]
                out[:, base + cut : base + units] = gate[:, first + cut : first + units]
                out[:, base + units : base + 2 * units - cut] = up[:, first + cut : first + units]
                out[:, base + 2 * units - cut : base + 2 * units] = up[:, first : first + cut]


def norm_kernel(nx, rows, near, far, out):
    step_rows = 32
    width = near.shape[1]
    x, c = lax.axis_index("mp") // 2, lax.axis_index("mp") % 2
    parity = lax.axis_index("section") % 2
    sides = []
    for ref, core in ((near, c), (far, 1 - c)):
        for k, step in enumerate((0, -1, 1, 2)):
            place = lax.rem(x + step + nx, nx) * 2 + core
            at = pl.ds(pl.multiple_of(place * width, width), width)
            sides.append((ref, k * (rows + 16), at))
    gains = [ref[first + rows : first + rows + 1, :].astype(jnp.float32) for ref, first, _ in sides]
    for mate in range(2):
        base = mate * 4 * (rows + 16)
        target_base = (1 - parity if mate else parity) * rows

        def body(i, carry, base=base, target_base=target_base):
            start = i * step_rows
            total = jnp.zeros((step_rows, width), jnp.float32)
            for ref, first, _ in sides:
                v = ref[pl.ds(pl.multiple_of(base + first + start, 16), step_rows), :].astype(jnp.float32)
                total = total + v * v
            scale = lax.rsqrt(jnp.sum(total, axis=1, keepdims=True) / (len(sides) * width) + 1e-06)
            target = pl.ds(pl.multiple_of(target_base + start, step_rows), step_rows)
            for (ref, first, at), gain in zip(sides, gains):
                v = ref[pl.ds(pl.multiple_of(base + first + start, 16), step_rows), :].astype(jnp.float32)
                out[target, at] = (v * scale * gain).astype(jnp.bfloat16)
            return carry

        lax.fori_loop(0, rows // step_rows, body, 0)


def marks(owner, shard_n):
    count = owner.shape[1]
    hit = lax.broadcasted_iota(jnp.int32, (shard_n, count), 0) == owner
    place = lax.broadcasted_iota(jnp.int32, (shard_n, count), 1).astype(jnp.float32)
    first = jnp.min(jnp.where(hit, place, 2.0 * count), axis=1, keepdims=True)
    last = jnp.max(jnp.where(hit, place, -1.0), axis=1, keepdims=True)
    return jnp.where(hit & (place == first), 1.0, 0.0), jnp.where(hit & (place == last) & (last > first), 1.0, 0.0)


def ask_kernel(owner, row, out):
    first, second = marks(owner[...], out.shape[0])
    wanted = row[...].astype(jnp.float32)
    one = jnp.sum(first * wanted, axis=1, keepdims=True)
    two = jnp.sum(second * wanted, axis=1, keepdims=True)
    lane = lax.broadcasted_iota(jnp.int32, out.shape, 1)
    out[...] = jnp.where(lane == 0, one, jnp.where(lane == 1, two, 0.0)).astype(jnp.int32)


def find_kernel(wanted, index, out):
    width, count = index.shape
    row = lax.broadcasted_iota(jnp.int32, (wanted.shape[0], count), 1)
    gap = jnp.zeros((wanted.shape[0], 128 - width), jnp.float32)
    for slot in range(2):
        hit = jnp.where(row == wanted[:, slot : slot + 1], 1.0, 0.0).astype(jnp.bfloat16)
        found = lax.dot_general(hit, index[...], (((1,), (1,)), ((), ())), preferred_element_type=jnp.float32)
        out[:, slot, :] = jnp.concatenate([found, gap], axis=1)


def hidden_kernel(units, normed, pool, weights, out, up_w, down_w, hidden, sems):
    h = lax.axis_index("dp") // (lax.axis_size("dp") // 2)
    rows = weights.shape[0]
    parts = 4
    piece = rows // parts
    copies = []
    for side, target in ((0, up_w), (2, up_w), (1, down_w)):
        base = rows if side == 2 else 0
        copies.append(
            [
                pltpu.make_async_copy(
                    weights.at[pl.ds(k * piece, piece), pl.ds(2 * units * side, 2 * units)],
                    target.at[pl.ds(base + k * piece, piece), :],
                    sems.at[side * parts + k],
                )
                for k in range(parts)
            ]
        )
    for group in copies:
        for copy in group:
            copy.start()
    cut = units // 128 * 128
    tail = units - cut
    tokens = normed.shape[0] // 2
    for part in range(2):
        at = slice(part * tokens, (part + 1) * tokens)
        both = None
        for side in range(2):
            if part == 0:
                for copy in copies[side]:
                    copy.wait()
            columns = pl.ds(pl.multiple_of((1 - h if side else h) * rows, rows), rows)
            term = jnp.dot(
                normed[at, columns], up_w[side * rows : (side + 1) * rows, :], preferred_element_type=jnp.float32
            )
            both = term if both is None else both + term
        hidden[at, :cut] = (gelu(both[:, :cut]) * both[:, 2 * units - cut :]).astype(jnp.bfloat16)
        if tail:
            edge = both[:, cut : cut + 2 * tail]
            hidden[at, cut : cut + 2 * tail] = (gelu(edge) * pltpu.roll(edge, tail, 1)).astype(jnp.bfloat16)
    value = jnp.dot(pool[...], hidden[...], preferred_element_type=jnp.float32)[:, :units]
    high = value.astype(jnp.bfloat16).astype(jnp.float32)
    low = value - high
    both_parts = jnp.concatenate([high, low], axis=0)
    none = jnp.zeros_like(both_parts)
    own_rows = jnp.concatenate([both_parts, none], axis=1)
    other_rows = jnp.concatenate([none, both_parts], axis=1)
    sides = jnp.concatenate([own_rows, other_rows], axis=0).astype(jnp.bfloat16)
    for copy in copies[2]:
        copy.wait()
    total = lax.dot_general(sides, down_w[...], (((1,), (1,)), ((), ())), preferred_element_type=jnp.float32)
    mp_n, _, width = out.shape[0] // 2, out.shape[1], out.shape[2]
    for side in range(2):
        sums = total[side * 32 : side * 32 + 16] + total[side * 32 + 16 : side * 32 + 32]
        for mate in range(2):
            base = mate * mp_n + (1 - h if side else h) * (mp_n // 2)
            for k in range(mp_n // 2):
                out[base + k] = sums[mate * 8 : mate * 8 + 8, k * width : (k + 1) * width]


def head_kernel(p_count, lanes, parts, residual, old_head, new_head, owner, fetched, pooled_out, message, old, new, sems):
    fetches = [pltpu.make_async_copy(old_head, old, sems.at[0]), pltpu.make_async_copy(new_head, new, sems.at[1])]
    for fetch in fetches:
        fetch.start()
    total = residual[...]
    for k in range(parts.shape[0]):
        total = total + parts[k]
    pooled = total.astype(jnp.bfloat16)
    pooled_out[...] = pooled
    for fetch in fetches:
        fetch.wait()
    of_old = jnp.dot(pooled, old[...], preferred_element_type=jnp.float32)
    of_new = jnp.dot(pooled, new[...], preferred_element_type=jnp.float32)
    row = lax.broadcasted_iota(jnp.int32, of_old.shape, 0)
    term = jnp.where(row < p_count, of_old, of_new)
    gap = jnp.zeros((term.shape[0], 128 - lanes), jnp.float32)
    pieces = [
        jnp.concatenate([term[:, k * lanes : (k + 1) * lanes], gap], axis=1) for k in range(term.shape[1] // lanes)
    ]
    negatives = jnp.zeros((owner.shape[1], 128), jnp.float32)
    for slot, mark in enumerate(marks(owner[...], fetched.shape[0])):
        negatives = negatives + lax.dot_general(
            mark.astype(jnp.bfloat16),
            fetched[:, slot, :].astype(jnp.bfloat16),
            (((0,), (0,)), ((), ())),
            preferred_element_type=jnp.float32,
        )
    rows = jnp.concatenate(pieces + [negatives], axis=0).astype(jnp.bfloat16)
    for copy in range(message.shape[0]):
        message[copy] = rows


def loss_kernel(p_count, q_count, queries, slot, messages, pooled, fresh_out, loss_out, message, held):
    n = messages.shape[0]
    rows = messages[...].astype(jnp.float32)
    total = rows[0, : n * 8]
    for k in range(1, n):
        total = total + rows[k, : n * 8]
    emb = jnp.concatenate([total[a * 8 : (a + 1) * 8] for a in range(n)], axis=1)
    fresh = emb[:p_count].astype(jnp.bfloat16).astype(jnp.float32)
    held[:p_count] = fresh
    own = held[:, pl.ds(pl.multiple_of(lax.axis_index("mp") * 128, 128), 128)]
    fresh_out[...] = own[:p_count, : fresh_out.shape[1]].astype(jnp.bfloat16)
    k_count = (rows.shape[1] - n * 8) // q_count
    loss_rows, grad_rows = [], []
    for q in range(q_count):
        query = emb[p_count + q : p_count + q + 1]
        positive = fresh[0:1]
        for k in range(1, p_count):
            positive = jnp.where(slot[q] == k, fresh[k : k + 1], positive)
        tiles = [rows[a, n * 8 + q * k_count : n * 8 + (q + 1) * k_count] for a in range(n)]
        inner = jnp.zeros((k_count, 128), jnp.float32)
        square = inner
        for a in range(n):
            inner = inner + tiles[a] * query[:, a * 128 : (a + 1) * 128]
            square = square + tiles[a] * tiles[a]
        inner = jnp.sum(inner, axis=1, keepdims=True)
        square = jnp.sum(square, axis=1, keepdims=True)
        query_norm = jnp.sqrt(jnp.sum(query * query, axis=1, keepdims=True) + 1e-06)
        below = jnp.sqrt(square + 1e-06) * query_norm * TAU
        scores = inner / below
        below_p = jnp.sqrt(jnp.sum(positive * positive, axis=1, keepdims=True) + 1e-06) * query_norm * TAU
        score_p = jnp.sum(positive * query, axis=1, keepdims=True) / below_p
        exps, exp_p = jnp.exp(scores), jnp.exp(score_p)
        total = jnp.sum(exps, axis=0, keepdims=True) + exp_p
        loss_rows.append(jnp.log(total) - score_p)
        weights = exps / total / queries
        weight_p = (exp_p / total - 1.0) / queries
        radial = (jnp.sum(weights * scores, axis=0, keepdims=True) + weight_p * score_p) / (query_norm * query_norm)
        share = weights / below
        direct = jnp.concatenate([jnp.sum(share * tile, axis=0, keepdims=True) for tile in tiles], axis=1)
        grad_rows.append(direct + (weight_p / below_p) * positive - radial * query)
    losses = jnp.concatenate(loss_rows, axis=0)
    loss_out[...] = jnp.broadcast_to(losses, loss_out.shape)
    grads = jnp.concatenate(grad_rows, axis=0).astype(jnp.bfloat16)
    width = pooled.shape[1]
    features = pooled[...].astype(jnp.float32)[p_count : p_count + q_count].astype(jnp.bfloat16)
    columns = lax.axis_size("dp")
    for k in range(message.shape[0]):
        at = k % columns * n // columns * 128
        message[k, :, :width] = features
        message[k, :, width:] = grads[:, at : at + 128]


def grad_kernel(width, arrived, out):
    block = out.shape[0]
    both = lax.dot_general(
        arrived[:, width:], arrived[:, :width], (((0,), (0,)), ((), ())), preferred_element_type=jnp.float32
    )
    shared = lax.axis_size("dp") // lax.axis_size("mp")
    chosen = both[:block]
    for k in range(1, shared):
        chosen = jnp.where(lax.axis_index("dp") % shared == k, both[k * block : (k + 1) * block], chosen)
    out[...] = chosen


def shards(
    passage_tokens,
    query_tokens,
    norm_gain,
    w_gate,
    w_up,
    w_down,
    old_head,
    new_head,
    stale_index,
    neg_owner,
    neg_row,
    pos_slot,
):
    p_count, length, width = passage_tokens.shape
    q_count, q_length, _ = query_tokens.shape
    k_count = neg_owner.shape[1]
    embed = old_head.shape[1]
    sections = lax.axis_size("section")
    shard_count = sections * lax.axis_size("dp")
    mp_n = lax.axis_size("mp")
    features = width * mp_n
    f32, bf16 = jnp.float32, jnp.bfloat16

    units = w_gate.shape[1] // 2
    cut = units // 128 * 128
    wide = -(-3 * units // 128) * 128
    own, other = pl.pallas_call(
        cut_kernel,
        out_shape=[jax.ShapeDtypeStruct((w_gate.shape[0], wide), bf16)] * 2,
        in_specs=[in_hbm()] * 3,
        out_specs=[whole()] * 2,
        scratch_shapes=[pltpu.VMEM(w.shape, bf16) for w in (w_gate, w_up, w_down)] + [pltpu.SemaphoreType.DMA((3,))],
        compiler_params=params(56),
        name="cut",
    )(w_gate, w_up, w_down)
    other = half_move(other)

    rows = p_count * length + q_count * q_length
    gain_rows = jnp.broadcast_to(norm_gain[None, :], (16, width))
    tokens = jnp.concatenate(
        [passage_tokens.reshape(-1, width), query_tokens.reshape(-1, width), gain_rows], axis=0
    )
    request_count = q_count * k_count
    owner = neg_owner.reshape(1, request_count)
    requests = pl.pallas_call(
        ask_kernel,
        out_shape=jax.ShapeDtypeStruct((shard_count, 128), jnp.int32),
        in_specs=[whole()] * 2,
        out_specs=whole(),
        compiler_params=params(),
        name="ask",
    )(owner, neg_row.reshape(1, request_count))

    low, high = mp_move(tokens, 1, 0), mp_move(tokens, -1, 0)
    other, requests, low, high = lax.optimization_barrier((other, requests, low, high))
    gap = 6 * units - wide
    weights = along_y(jnp.pad(own, ((0, 0), (0, gap))) + jnp.pad(other, ((0, 0), (gap, 0))))

    wanted = lax.all_to_all(requests, ("section", "dp"), 0, 0, tiled=True)
    near, far, wanted = spread(tokens, low, high, wanted)
    found = pl.pallas_call(
        find_kernel,
        out_shape=jax.ShapeDtypeStruct((shard_count, 2, 128), f32),
        in_specs=[whole()] * 2,
        out_specs=whole(),
        compiler_params=params(),
        name="find",
    )(wanted, stale_index.T)
    fetched = lax.all_to_all(found, ("section", "dp"), 0, 0, tiled=True)

    normed = pl.pallas_call(
        functools.partial(norm_kernel, mp_n // 2, rows),
        out_shape=jax.ShapeDtypeStruct((2 * rows, features), bf16),
        in_specs=[whole()] * 2,
        out_specs=whole(),
        compiler_params=params(16),
        name="norm",
    )(near, far)

    pool = np.zeros((16, 2 * rows), np.float32)
    for mate in range(2):
        base = mate * rows
        for k in range(p_count):
            pool[mate * 8 + k, base + k * length : base + (k + 1) * length] = 1.0 / length
        base += p_count * length
        for k in range(q_count):
            pool[mate * 8 + p_count + k, base + k * q_length : base + (k + 1) * q_length] = 1.0 / q_length
    padded = cut + 2 * (units - cut)
    parts = pl.pallas_call(
        functools.partial(hidden_kernel, units),
        out_shape=jax.ShapeDtypeStruct((2 * mp_n, 8, width), f32),
        in_specs=[whole(), whole(), in_hbm()],
        out_specs=whole(),
        scratch_shapes=[
            pltpu.VMEM((features, 2 * units), bf16),
            pltpu.VMEM((features // 2, 2 * units), bf16),
            pltpu.VMEM((2 * rows, padded), bf16),
            pltpu.SemaphoreType.DMA((12,)),
        ],
        compiler_params=params(52),
        name="hidden",
    )(normed, jnp.asarray(pool, bf16), weights)

    groups = [[s * mp_n + m for s in (p, p + 1) for m in range(mp_n)] for p in range(0, sections, 2)]
    parts = lax.all_to_all(
        parts, ("section", "mp"), split_axis=0, concat_axis=0, axis_index_groups=groups, tiled=True
    )
    residual = jnp.concatenate(
        [
            jnp.sum(passage_tokens.astype(f32), axis=1) / length,
            jnp.sum(query_tokens.astype(f32), axis=1) / q_length,
            jnp.zeros((8 - p_count - q_count, width), f32),
        ],
        axis=0,
    )
    own_width = embed // mp_n
    message_rows = 8 * mp_n + request_count
    pooled, message = pl.pallas_call(
        functools.partial(head_kernel, p_count, own_width),
        out_shape=[
            jax.ShapeDtypeStruct((8, width), bf16),
            jax.ShapeDtypeStruct((mp_n, message_rows, 128), bf16),
        ],
        in_specs=[whole()] * 2 + [in_hbm()] * 2 + [whole()] * 2,
        out_specs=[whole()] * 2,
        scratch_shapes=[
            pltpu.VMEM((width, embed), bf16),
            pltpu.VMEM((width, embed), bf16),
            pltpu.SemaphoreType.DMA((2,)),
        ],
        compiler_params=params(),
        name="head",
    )(parts, residual, old_head, new_head, owner, fetched)
    messages = lax.all_to_all(message, "mp", 0, 0, tiled=True)

    refreshed, losses, message = pl.pallas_call(
        functools.partial(loss_kernel, p_count, q_count, q_count * shard_count),
        out_shape=[
            jax.ShapeDtypeStruct((p_count, own_width), bf16),
            jax.ShapeDtypeStruct((q_count, 128), f32),
            jax.ShapeDtypeStruct((shard_count, q_count, width + 128), bf16),
        ],
        in_specs=[pl.BlockSpec(memory_space=pltpu.SMEM)] + [whole()] * 2,
        out_specs=[whole()] * 3,
        scratch_shapes=[pltpu.VMEM((8, 128 * mp_n), f32)],
        compiler_params=params(),
        name="loss",
    )(pos_slot, messages, pooled)

    arrived = lax.all_to_all(message, ("section", "dp"), 0, 0, tiled=True)
    head_grad = pl.pallas_call(
        functools.partial(grad_kernel, width),
        out_shape=jax.ShapeDtypeStruct((embed // lax.axis_size("dp"), width), f32),
        in_specs=[whole()],
        out_specs=whole(),
        compiler_params=params(),
        name="grad",
    )(arrived.reshape(-1, width + 128)).T
    return (refreshed, losses[:, 0], head_grad)


def solution(mesh):
    placed = (
        P(("section", "dp"), None, "mp"),
        P(("section", "dp"), None, "mp"),
        P("mp"),
        P("dp", "mp"),
        P("dp", "mp"),
        P("mp", "dp"),
        P("mp", None),
        P("mp", None),
        P(("section", "dp"), "mp"),
        P(("section", "dp"), None),
        P(("section", "dp"), None),
        P(("section", "dp")),
    )
    return jax.shard_map(
        shards,
        mesh=mesh,
        in_specs=placed,
        out_specs=(P(("section", "dp"), "mp"), P(("section", "dp")), P("mp", "dp")),
        check_vma=False,
    )
```

```python
import functools
import math

import jax
import jax.numpy as jnp
import numpy as np
from jax import lax
from jax.experimental import pallas as pl
from jax.experimental.pallas import tpu as pltpu
from jax.sharding import PartitionSpec as P

TAU = 0.02
MIB = 1024 * 1024


def params(mib=8):
    return pltpu.CompilerParams(vmem_limit_bytes=mib * MIB)


def in_hbm():
    return pl.BlockSpec(memory_space=pltpu.HBM)


def whole():
    return pl.BlockSpec(memory_space=pltpu.VMEM)


def gelu(v):
    c = math.sqrt(2.0 / math.pi)
    return 0.5 * v * (1.0 + jnp.tanh(c * (v + 0.044715 * (v * v * v))))


def mp_move(block, step, flip):
    n = lax.axis_size("mp") // 2
    perm = [(x * 2 + c, ((x + step) % n) * 2 + (c ^ flip)) for x in range(n) for c in range(2)]
    return lax.ppermute(block, "mp", perm)


def mate_move(block):
    return lax.ppermute(block, "section", [(s, s ^ 1) for s in range(lax.axis_size("section"))])


def half_move(block):
    sections, shards_n = lax.axis_size("section"), lax.axis_size("dp")
    turn = sections // 2 if (sections // 2) % 2 == 0 else 0
    perm = [
        (s * shards_n + d, ((s + turn) % sections) * shards_n + (d + shards_n // 2) % shards_n)
        for s in range(sections)
        for d in range(shards_n)
    ]
    return lax.ppermute(block, ("section", "dp"), perm)


def along_y(block):
    n = lax.axis_size("dp") // 2
    groups = [[h * n + y for y in range(n)] for h in range(2)]
    return lax.all_gather(block, "dp", axis=0, axis_index_groups=groups, tiled=True)


def spread(block, low, high, wanted):
    mine = jnp.concatenate([block, low, high, mp_move(block, 2, 0)], axis=0)
    mate, wanted = lax.optimization_barrier((mate_move(mine), wanted))
    mine = jnp.concatenate([mine, mate], axis=0)
    return mine, mp_move(mine, 0, 1), wanted


def cut_kernel(gate_in, up_in, down_in, own, other, gate, up, down, sems):
    fetches = [
        pltpu.make_async_copy(source, target, sems.at[k])
        for k, (source, target) in enumerate(((gate_in, gate), (up_in, up), (down_in, down)))
    ]
    for fetch in fetches:
        fetch.start()
    units = gate.shape[1] // 2
    cut = units // 128 * 128
    gap = other.shape[1] - 3 * units
    own[:, 3 * units :] = jnp.zeros((own.shape[0], own.shape[1] - 3 * units), own.dtype)
    other[:, :gap] = jnp.zeros((own.shape[0], gap), own.dtype)
    for fetch in fetches:
        fetch.wait()
    for half in range(2):

        @pl.when(lax.axis_index("section") % 2 == half)
        def _(first=half * units):
            turned = down[first : first + units, :].astype(jnp.float32).T.astype(jnp.bfloat16)
            own[:, 2 * units : 3 * units] = turned
            other[:, gap : gap + units] = turned
            for out, base in ((own, 0), (other, gap + units)):
                out[:, base : base + cut] = gate[:, first : first + cut]
                out[:, base + cut : base + units] = gate[:, first + cut : first + units]
                out[:, base + units : base + 2 * units - cut] = up[:, first + cut : first + units]
                out[:, base + 2 * units - cut : base + 2 * units] = up[:, first : first + cut]


def norm_kernel(nx, rows, near, far, out):
    step_rows = 32
    width = near.shape[1]
    x, c = lax.axis_index("mp") // 2, lax.axis_index("mp") % 2
    parity = lax.axis_index("section") % 2
    sides = []
    for ref, core in ((near, c), (far, 1 - c)):
        for k, step in enumerate((0, -1, 1, 2)):
            place = lax.rem(x + step + nx, nx) * 2 + core
            at = pl.ds(pl.multiple_of(place * width, width), width)
            sides.append((ref, k * (rows + 16), at))
    gains = [ref[first + rows : first + rows + 1, :].astype(jnp.float32) for ref, first, _ in sides]
    for mate in range(2):
        base = mate * 4 * (rows + 16)
        target_base = (1 - parity if mate else parity) * rows

        def body(i, carry, base=base, target_base=target_base):
            start = i * step_rows
            total = jnp.zeros((step_rows, width), jnp.float32)
            for ref, first, _ in sides:
                v = ref[pl.ds(pl.multiple_of(base + first + start, 16), step_rows), :].astype(jnp.float32)
                total = total + v * v
            scale = lax.rsqrt(jnp.sum(total, axis=1, keepdims=True) / (len(sides) * width) + 1e-06)
            target = pl.ds(pl.multiple_of(target_base + start, step_rows), step_rows)
            for (ref, first, at), gain in zip(sides, gains):
                v = ref[pl.ds(pl.multiple_of(base + first + start, 16), step_rows), :].astype(jnp.float32)
                out[target, at] = (v * scale * gain).astype(jnp.bfloat16)
            return carry

        lax.fori_loop(0, rows // step_rows, body, 0)


def marks(owner, shard_n):
    count = owner.shape[1]
    hit = lax.broadcasted_iota(jnp.int32, (shard_n, count), 0) == owner
    place = lax.broadcasted_iota(jnp.int32, (shard_n, count), 1).astype(jnp.float32)
    first = jnp.min(jnp.where(hit, place, 2.0 * count), axis=1, keepdims=True)
    last = jnp.max(jnp.where(hit, place, -1.0), axis=1, keepdims=True)
    return jnp.where(hit & (place == first), 1.0, 0.0), jnp.where(hit & (place == last) & (last > first), 1.0, 0.0)


def ask_kernel(owner, row, out):
    first, second = marks(owner[...], out.shape[0])
    wanted = row[...].astype(jnp.float32)
    one = jnp.sum(first * wanted, axis=1, keepdims=True)
    two = jnp.sum(second * wanted, axis=1, keepdims=True)
    lane = lax.broadcasted_iota(jnp.int32, out.shape, 1)
    out[...] = jnp.where(lane == 0, one, jnp.where(lane == 1, two, 0.0)).astype(jnp.int32)


def find_kernel(wanted, index, out):
    width, count = index.shape
    row = lax.broadcasted_iota(jnp.int32, (wanted.shape[0], count), 1)
    gap = jnp.zeros((wanted.shape[0], 128 - width), jnp.float32)
    for slot in range(2):
        hit = jnp.where(row == wanted[:, slot : slot + 1], 1.0, 0.0).astype(jnp.bfloat16)
        found = lax.dot_general(hit, index[...], (((1,), (1,)), ((), ())), preferred_element_type=jnp.float32)
        out[:, slot, :] = jnp.concatenate([found, gap], axis=1)


def hidden_kernel(units, normed, pool, weights, out, up_w, down_w, hidden, sems):
    h = lax.axis_index("dp") // (lax.axis_size("dp") // 2)
    rows = weights.shape[0]
    parts = 4
    piece = rows // parts
    copies = []
    for side, target in ((0, up_w), (2, up_w), (1, down_w)):
        base = rows if side == 2 else 0
        copies.append(
            [
                pltpu.make_async_copy(
                    weights.at[pl.ds(k * piece, piece), pl.ds(2 * units * side, 2 * units)],
                    target.at[pl.ds(base + k * piece, piece), :],
                    sems.at[side * parts + k],
                )
                for k in range(parts)
            ]
        )
    for group in copies:
        for copy in group:
            copy.start()
    cut = units // 128 * 128
    tail = units - cut
    tokens = normed.shape[0] // 2
    for part in range(2):
        at = slice(part * tokens, (part + 1) * tokens)
        both = None
        for side in range(2):
            if part == 0:
                for copy in copies[side]:
                    copy.wait()
            columns = pl.ds(pl.multiple_of((1 - h if side else h) * rows, rows), rows)
            term = jnp.dot(
                normed[at, columns], up_w[side * rows : (side + 1) * rows, :], preferred_element_type=jnp.float32
            )
            both = term if both is None else both + term
        hidden[at, :cut] = (gelu(both[:, :cut]) * both[:, 2 * units - cut :]).astype(jnp.bfloat16)
        if tail:
            edge = both[:, cut : cut + 2 * tail]
            hidden[at, cut : cut + 2 * tail] = (gelu(edge) * pltpu.roll(edge, tail, 1)).astype(jnp.bfloat16)
    value = jnp.dot(pool[...], hidden[...], preferred_element_type=jnp.float32)[:, :units]
    high = value.astype(jnp.bfloat16).astype(jnp.float32)
    low = value - high
    both_parts = jnp.concatenate([high, low], axis=0)
    none = jnp.zeros_like(both_parts)
    own_rows = jnp.concatenate([both_parts, none], axis=1)
    other_rows = jnp.concatenate([none, both_parts], axis=1)
    sides = jnp.concatenate([own_rows, other_rows], axis=0).astype(jnp.bfloat16)
    for copy in copies[2]:
        copy.wait()
    total = lax.dot_general(sides, down_w[...], (((1,), (1,)), ((), ())), preferred_element_type=jnp.float32)
    mp_n, _, width = out.shape[0] // 2, out.shape[1], out.shape[2]
    for side in range(2):
        sums = total[side * 32 : side * 32 + 16] + total[side * 32 + 16 : side * 32 + 32]
        for mate in range(2):
            base = mate * mp_n + (1 - h if side else h) * (mp_n // 2)
            for k in range(mp_n // 2):
                out[base + k] = sums[mate * 8 : mate * 8 + 8, k * width : (k + 1) * width]


def head_kernel(p_count, lanes, parts, residual, old_head, new_head, owner, fetched, pooled_out, message, old, new, sems):
    fetches = [pltpu.make_async_copy(old_head, old, sems.at[0]), pltpu.make_async_copy(new_head, new, sems.at[1])]
    for fetch in fetches:
        fetch.start()
    total = residual[...]
    for k in range(parts.shape[0]):
        total = total + parts[k]
    pooled = total.astype(jnp.bfloat16)
    pooled_out[...] = pooled
    for fetch in fetches:
        fetch.wait()
    of_old = jnp.dot(pooled, old[...], preferred_element_type=jnp.float32)
    of_new = jnp.dot(pooled, new[...], preferred_element_type=jnp.float32)
    row = lax.broadcasted_iota(jnp.int32, of_old.shape, 0)
    term = jnp.where(row < p_count, of_old, of_new)
    gap = jnp.zeros((term.shape[0], 128 - lanes), jnp.float32)
    pieces = [
        jnp.concatenate([term[:, k * lanes : (k + 1) * lanes], gap], axis=1) for k in range(term.shape[1] // lanes)
    ]
    negatives = jnp.zeros((owner.shape[1], 128), jnp.float32)
    for slot, mark in enumerate(marks(owner[...], fetched.shape[0])):
        negatives = negatives + lax.dot_general(
            mark.astype(jnp.bfloat16),
            fetched[:, slot, :].astype(jnp.bfloat16),
            (((0,), (0,)), ((), ())),
            preferred_element_type=jnp.float32,
        )
    rows = jnp.concatenate(pieces + [negatives], axis=0).astype(jnp.bfloat16)
    for copy in range(message.shape[0]):
        message[copy] = rows


def loss_kernel(p_count, q_count, queries, slot, messages, pooled, fresh_out, loss_out, message, held):
    n = messages.shape[0]
    rows = messages[...].astype(jnp.float32)
    total = rows[0, : n * 8]
    for k in range(1, n):
        total = total + rows[k, : n * 8]
    emb = jnp.concatenate([total[a * 8 : (a + 1) * 8] for a in range(n)], axis=1)
    fresh = emb[:p_count].astype(jnp.bfloat16).astype(jnp.float32)
    held[:p_count] = fresh
    own = held[:, pl.ds(pl.multiple_of(lax.axis_index("mp") * 128, 128), 128)]
    fresh_out[...] = own[:p_count, : fresh_out.shape[1]].astype(jnp.bfloat16)
    k_count = (rows.shape[1] - n * 8) // q_count
    loss_rows, grad_rows = [], []
    for q in range(q_count):
        query = emb[p_count + q : p_count + q + 1]
        positive = fresh[0:1]
        for k in range(1, p_count):
            positive = jnp.where(slot[q] == k, fresh[k : k + 1], positive)
        tiles = [rows[a, n * 8 + q * k_count : n * 8 + (q + 1) * k_count] for a in range(n)]
        inner = jnp.zeros((k_count, 128), jnp.float32)
        square = inner
        for a in range(n):
            inner = inner + tiles[a] * query[:, a * 128 : (a + 1) * 128]
            square = square + tiles[a] * tiles[a]
        inner = jnp.sum(inner, axis=1, keepdims=True)
        square = jnp.sum(square, axis=1, keepdims=True)
        query_norm = jnp.sqrt(jnp.sum(query * query, axis=1, keepdims=True) + 1e-06)
        below = jnp.sqrt(square + 1e-06) * query_norm * TAU
        scores = inner / below
        below_p = jnp.sqrt(jnp.sum(positive * positive, axis=1, keepdims=True) + 1e-06) * query_norm * TAU
        score_p = jnp.sum(positive * query, axis=1, keepdims=True) / below_p
        exps, exp_p = jnp.exp(scores), jnp.exp(score_p)
        total = jnp.sum(exps, axis=0, keepdims=True) + exp_p
        loss_rows.append(jnp.log(total) - score_p)
        weights = exps / total / queries
        weight_p = (exp_p / total - 1.0) / queries
        radial = (jnp.sum(weights * scores, axis=0, keepdims=True) + weight_p * score_p) / (query_norm * query_norm)
        share = weights / below
        direct = jnp.concatenate([jnp.sum(share * tile, axis=0, keepdims=True) for tile in tiles], axis=1)
        grad_rows.append(direct + (weight_p / below_p) * positive - radial * query)
    losses = jnp.concatenate(loss_rows, axis=0)
    loss_out[...] = jnp.broadcast_to(losses, loss_out.shape)
    grads = jnp.concatenate(grad_rows, axis=0).astype(jnp.bfloat16)
    width = pooled.shape[1]
    features = pooled[...].astype(jnp.float32)[p_count : p_count + q_count].astype(jnp.bfloat16)
    columns = lax.axis_size("dp")
    for k in range(message.shape[0]):
        at = k % columns * n // columns * 128
        message[k, :, :width] = features
        message[k, :, width:] = grads[:, at : at + 128]


def grad_kernel(width, arrived, out):
    block = out.shape[0]
    both = lax.dot_general(
        arrived[:, width:], arrived[:, :width], (((0,), (0,)), ((), ())), preferred_element_type=jnp.float32
    )
    shared = lax.axis_size("dp") // lax.axis_size("mp")
    chosen = both[:block]
    for k in range(1, shared):
        chosen = jnp.where(lax.axis_index("dp") % shared == k, both[k * block : (k + 1) * block], chosen)
    out[...] = chosen


def shards(
    passage_tokens,
    query_tokens,
    norm_gain,
    w_gate,
    w_up,
    w_down,
    old_head,
    new_head,
    stale_index,
    neg_owner,
    neg_row,
    pos_slot,
):
    p_count, length, width = passage_tokens.shape
    q_count, q_length, _ = query_tokens.shape
    k_count = neg_owner.shape[1]
    embed = old_head.shape[1]
    sections = lax.axis_size("section")
    shard_count = sections * lax.axis_size("dp")
    mp_n = lax.axis_size("mp")
    features = width * mp_n
    f32, bf16 = jnp.float32, jnp.bfloat16

    units = w_gate.shape[1] // 2
    cut = units // 128 * 128
    wide = -(-3 * units // 128) * 128
    own, other = pl.pallas_call(
        cut_kernel,
        out_shape=[jax.ShapeDtypeStruct((w_gate.shape[0], lanes), bf16) for lanes in (6 * units, wide)],
        in_specs=[in_hbm()] * 3,
        out_specs=[whole()] * 2,
        scratch_shapes=[pltpu.VMEM(w.shape, bf16) for w in (w_gate, w_up, w_down)] + [pltpu.SemaphoreType.DMA((3,))],
        compiler_params=params(56),
        name="cut",
    )(w_gate, w_up, w_down)
    other = half_move(other)

    rows = p_count * length + q_count * q_length
    gain_rows = jnp.broadcast_to(norm_gain[None, :], (16, width))
    tokens = jnp.concatenate(
        [passage_tokens.reshape(-1, width), query_tokens.reshape(-1, width), gain_rows], axis=0
    )
    request_count = q_count * k_count
    owner = neg_owner.reshape(1, request_count)
    requests = pl.pallas_call(
        ask_kernel,
        out_shape=jax.ShapeDtypeStruct((shard_count, 128), jnp.int32),
        in_specs=[whole()] * 2,
        out_specs=whole(),
        compiler_params=params(),
        name="ask",
    )(owner, neg_row.reshape(1, request_count))

    low, high = mp_move(tokens, 1, 0), mp_move(tokens, -1, 0)
    other, requests, low = lax.optimization_barrier((other, requests, low))
    edge = 6 * units - wide
    weights = along_y(lax.dynamic_update_slice(own, own[:, edge:] + other, (0, edge)))

    wanted = lax.all_to_all(requests, ("section", "dp"), 0, 0, tiled=True)
    near, far, wanted = spread(tokens, low, high, wanted)
    found = pl.pallas_call(
        find_kernel,
        out_shape=jax.ShapeDtypeStruct((shard_count, 2, 128), f32),
        in_specs=[whole()] * 2,
        out_specs=whole(),
        compiler_params=params(),
        name="find",
    )(wanted, stale_index.T)
    fetched = lax.all_to_all(found, ("section", "dp"), 0, 0, tiled=True)

    normed = pl.pallas_call(
        functools.partial(norm_kernel, mp_n // 2, rows),
        out_shape=jax.ShapeDtypeStruct((2 * rows, features), bf16),
        in_specs=[whole()] * 2,
        out_specs=whole(),
        compiler_params=params(16),
        name="norm",
    )(near, far)

    pool = np.zeros((16, 2 * rows), np.float32)
    for mate in range(2):
        base = mate * rows
        for k in range(p_count):
            pool[mate * 8 + k, base + k * length : base + (k + 1) * length] = 1.0 / length
        base += p_count * length
        for k in range(q_count):
            pool[mate * 8 + p_count + k, base + k * q_length : base + (k + 1) * q_length] = 1.0 / q_length
    padded = cut + 2 * (units - cut)
    parts = pl.pallas_call(
        functools.partial(hidden_kernel, units),
        out_shape=jax.ShapeDtypeStruct((2 * mp_n, 8, width), f32),
        in_specs=[whole(), whole(), in_hbm()],
        out_specs=whole(),
        scratch_shapes=[
            pltpu.VMEM((features, 2 * units), bf16),
            pltpu.VMEM((features // 2, 2 * units), bf16),
            pltpu.VMEM((2 * rows, padded), bf16),
            pltpu.SemaphoreType.DMA((12,)),
        ],
        compiler_params=params(52),
        name="hidden",
    )(normed, jnp.asarray(pool, bf16), weights)

    groups = [[s * mp_n + m for s in (p, p + 1) for m in range(mp_n)] for p in range(0, sections, 2)]
    parts = lax.all_to_all(
        parts, ("section", "mp"), split_axis=0, concat_axis=0, axis_index_groups=groups, tiled=True
    )
    residual = jnp.concatenate(
        [
            jnp.sum(passage_tokens.astype(f32), axis=1) / length,
            jnp.sum(query_tokens.astype(f32), axis=1) / q_length,
            jnp.zeros((8 - p_count - q_count, width), f32),
        ],
        axis=0,
    )
    own_width = embed // mp_n
    message_rows = 8 * mp_n + request_count
    pooled, message = pl.pallas_call(
        functools.partial(head_kernel, p_count, own_width),
        out_shape=[
            jax.ShapeDtypeStruct((8, width), bf16),
            jax.ShapeDtypeStruct((mp_n, message_rows, 128), bf16),
        ],
        in_specs=[whole()] * 2 + [in_hbm()] * 2 + [whole()] * 2,
        out_specs=[whole()] * 2,
        scratch_shapes=[
            pltpu.VMEM((width, embed), bf16),
            pltpu.VMEM((width, embed), bf16),
            pltpu.SemaphoreType.DMA((2,)),
        ],
        compiler_params=params(),
        name="head",
    )(parts, residual, old_head, new_head, owner, fetched)
    messages = lax.all_to_all(message, "mp", 0, 0, tiled=True)

    refreshed, losses, message = pl.pallas_call(
        functools.partial(loss_kernel, p_count, q_count, q_count * shard_count),
        out_shape=[
            jax.ShapeDtypeStruct((p_count, own_width), bf16),
            jax.ShapeDtypeStruct((q_count, 128), f32),
            jax.ShapeDtypeStruct((shard_count, q_count, width + 128), bf16),
        ],
        in_specs=[pl.BlockSpec(memory_space=pltpu.SMEM)] + [whole()] * 2,
        out_specs=[whole()] * 3,
        scratch_shapes=[pltpu.VMEM((8, 128 * mp_n), f32)],
        compiler_params=params(),
        name="loss",
    )(pos_slot, messages, pooled)

    arrived = lax.all_to_all(message, ("section", "dp"), 0, 0, tiled=True)
    head_grad = pl.pallas_call(
        functools.partial(grad_kernel, width),
        out_shape=jax.ShapeDtypeStruct((embed // lax.axis_size("dp"), width), f32),
        in_specs=[whole()],
        out_specs=whole(),
        compiler_params=params(),
        name="grad",
    )(arrived.reshape(-1, width + 128)).T
    return (refreshed, losses[:, 0], head_grad)


def solution(mesh):
    placed = (
        P(("section", "dp"), None, "mp"),
        P(("section", "dp"), None, "mp"),
        P("mp"),
        P("dp", "mp"),
        P("dp", "mp"),
        P("mp", "dp"),
        P("mp", None),
        P("mp", None),
        P(("section", "dp"), "mp"),
        P(("section", "dp"), None),
        P(("section", "dp"), None),
        P(("section", "dp")),
    )
    return jax.shard_map(
        shards,
        mesh=mesh,
        in_specs=placed,
        out_specs=(P(("section", "dp"), "mp"), P(("section", "dp")), P("mp", "dp")),
        check_vma=False,
    )
```

```python
import functools
import math

import jax
import jax.numpy as jnp
import numpy as np
from jax import lax
from jax.experimental import pallas as pl
from jax.experimental.pallas import tpu as pltpu
from jax.sharding import PartitionSpec as P

TAU = 0.02
MIB = 1024 * 1024


def params(mib=8):
    return pltpu.CompilerParams(vmem_limit_bytes=mib * MIB)


def in_hbm():
    return pl.BlockSpec(memory_space=pltpu.HBM)


def whole():
    return pl.BlockSpec(memory_space=pltpu.VMEM)


def gelu(v):
    c = math.sqrt(2.0 / math.pi)
    return 0.5 * v * (1.0 + jnp.tanh(c * (v + 0.044715 * (v * v * v))))


def mp_move(block, step, flip):
    n = lax.axis_size("mp") // 2
    perm = [(x * 2 + c, ((x + step) % n) * 2 + (c ^ flip)) for x in range(n) for c in range(2)]
    return lax.ppermute(block, "mp", perm)


def mate_move(block):
    return lax.ppermute(block, "section", [(s, s ^ 1) for s in range(lax.axis_size("section"))])


def half_move(block):
    sections, shards_n = lax.axis_size("section"), lax.axis_size("dp")
    turn = sections // 2 if (sections // 2) % 2 == 0 else 0
    perm = [
        (s * shards_n + d, ((s + turn) % sections) * shards_n + (d + shards_n // 2) % shards_n)
        for s in range(sections)
        for d in range(shards_n)
    ]
    return lax.ppermute(block, ("section", "dp"), perm)


def along_y(block):
    n = lax.axis_size("dp") // 2
    groups = [[h * n + y for y in range(n)] for h in range(2)]
    return lax.all_gather(block, "dp", axis=0, axis_index_groups=groups, tiled=True)


def spread(block, low, high, wanted):
    mine = jnp.concatenate([block, low, high, mp_move(block, 2, 0)], axis=0)
    mate, wanted = lax.optimization_barrier((mate_move(mine), wanted))
    mine = jnp.concatenate([mine, mate], axis=0)
    return mine, mp_move(mine, 0, 1), wanted


def cut_kernel(gate_in, up_in, down_in, passages, queries, gain, own, other, tokens, gate, up, down, sems):
    split = passages.shape[0]
    rows = split + queries.shape[0]
    fetches = [
        pltpu.make_async_copy(source, target, sems.at[k])
        for k, (source, target) in enumerate(
            (
                (gate_in, gate),
                (up_in, up),
                (down_in, down),
                (passages, tokens.at[pl.ds(0, split), :]),
                (queries, tokens.at[pl.ds(split, rows - split), :]),
            )
        )
    ]
    for fetch in fetches:
        fetch.start()
    tokens[rows:, :] = jnp.broadcast_to(gain[...], (tokens.shape[0] - rows, tokens.shape[1]))
    units = gate.shape[1] // 2
    cut = units // 128 * 128
    gap = own.shape[1] - 3 * units
    own[:, 3 * units :] = jnp.zeros((own.shape[0], gap), own.dtype)
    other[:, :gap] = jnp.zeros((own.shape[0], gap), own.dtype)
    for fetch in fetches:
        fetch.wait()
    for half in range(2):

        @pl.when(lax.axis_index("section") % 2 == half)
        def _(first=half * units):
            turned = down[first : first + units, :].astype(jnp.float32).T.astype(jnp.bfloat16)
            own[:, 2 * units : 3 * units] = turned
            other[:, gap : gap + units] = turned
            for out, base in ((own, 0), (other, gap + units)):
                out[:, base : base + cut] = gate[:, first : first + cut]
                out[:, base + cut : base + units] = gate[:, first + cut : first + units]
                out[:, base + units : base + 2 * units - cut] = up[:, first + cut : first + units]
                out[:, base + 2 * units - cut : base + 2 * units] = up[:, first : first + cut]


def norm_kernel(nx, rows, near, far, out):
    step_rows = 32
    width = near.shape[1]
    x, c = lax.axis_index("mp") // 2, lax.axis_index("mp") % 2
    parity = lax.axis_index("section") % 2
    sides = []
    for ref, core in ((near, c), (far, 1 - c)):
        for k, step in enumerate((0, -1, 1, 2)):
            place = lax.rem(x + step + nx, nx) * 2 + core
            at = pl.ds(pl.multiple_of(place * width, width), width)
            sides.append((ref, k * (rows + 16), at))
    gains = [ref[first + rows : first + rows + 1, :].astype(jnp.float32) for ref, first, _ in sides]
    for mate in range(2):
        base = mate * 4 * (rows + 16)
        target_base = (1 - parity if mate else parity) * rows

        def body(i, carry, base=base, target_base=target_base):
            start = i * step_rows
            total = jnp.zeros((step_rows, width), jnp.float32)
            for ref, first, _ in sides:
                v = ref[pl.ds(pl.multiple_of(base + first + start, 16), step_rows), :].astype(jnp.float32)
                total = total + v * v
            scale = lax.rsqrt(jnp.sum(total, axis=1, keepdims=True) / (len(sides) * width) + 1e-06)
            target = pl.ds(pl.multiple_of(target_base + start, step_rows), step_rows)
            for (ref, first, at), gain in zip(sides, gains):
                v = ref[pl.ds(pl.multiple_of(base + first + start, 16), step_rows), :].astype(jnp.float32)
                out[target, at] = (v * scale * gain).astype(jnp.bfloat16)
            return carry

        lax.fori_loop(0, rows // step_rows, body, 0)


def marks(owner, shard_n):
    count = owner.shape[1]
    hit = lax.broadcasted_iota(jnp.int32, (shard_n, count), 0) == owner
    place = lax.broadcasted_iota(jnp.int32, (shard_n, count), 1).astype(jnp.float32)
    first = jnp.min(jnp.where(hit, place, 2.0 * count), axis=1, keepdims=True)
    last = jnp.max(jnp.where(hit, place, -1.0), axis=1, keepdims=True)
    return jnp.where(hit & (place == first), 1.0, 0.0), jnp.where(hit & (place == last) & (last > first), 1.0, 0.0)


def ask_kernel(owner, row, out):
    first, second = marks(owner[...], out.shape[0])
    wanted = row[...].astype(jnp.float32)
    one = jnp.sum(first * wanted, axis=1, keepdims=True)
    two = jnp.sum(second * wanted, axis=1, keepdims=True)
    lane = lax.broadcasted_iota(jnp.int32, out.shape, 1)
    out[...] = jnp.where(lane == 0, one, jnp.where(lane == 1, two, 0.0)).astype(jnp.int32)


def find_kernel(wanted, index, out):
    width, count = index.shape
    row = lax.broadcasted_iota(jnp.int32, (wanted.shape[0], count), 1)
    gap = jnp.zeros((wanted.shape[0], 128 - width), jnp.float32)
    for slot in range(2):
        hit = jnp.where(row == wanted[:, slot : slot + 1], 1.0, 0.0).astype(jnp.bfloat16)
        found = lax.dot_general(hit, index[...], (((1,), (1,)), ((), ())), preferred_element_type=jnp.float32)
        out[:, slot, :] = jnp.concatenate([found, gap], axis=1)


def hidden_kernel(units, normed, pool, weights, out, up_w, down_w, hidden, sems):
    h = lax.axis_index("dp") // (lax.axis_size("dp") // 2)
    rows = weights.shape[0]
    parts = 4
    piece = rows // parts
    copies = []
    for side, target in ((0, up_w), (2, up_w), (1, down_w)):
        base = rows if side == 2 else 0
        copies.append(
            [
                pltpu.make_async_copy(
                    weights.at[pl.ds(k * piece, piece), pl.ds(2 * units * side, 2 * units)],
                    target.at[pl.ds(base + k * piece, piece), :],
                    sems.at[side * parts + k],
                )
                for k in range(parts)
            ]
        )
    for group in copies:
        for copy in group:
            copy.start()
    cut = units // 128 * 128
    tail = units - cut
    tokens = normed.shape[0] // 2
    for part in range(2):
        at = slice(part * tokens, (part + 1) * tokens)
        both = None
        for side in range(2):
            if part == 0:
                for copy in copies[side]:
                    copy.wait()
            columns = pl.ds(pl.multiple_of((1 - h if side else h) * rows, rows), rows)
            term = jnp.dot(
                normed[at, columns], up_w[side * rows : (side + 1) * rows, :], preferred_element_type=jnp.float32
            )
            both = term if both is None else both + term
        hidden[at, :cut] = (gelu(both[:, :cut]) * both[:, 2 * units - cut :]).astype(jnp.bfloat16)
        if tail:
            edge = both[:, cut : cut + 2 * tail]
            hidden[at, cut : cut + 2 * tail] = (gelu(edge) * pltpu.roll(edge, tail, 1)).astype(jnp.bfloat16)
    value = jnp.dot(pool[...], hidden[...], preferred_element_type=jnp.float32)[:, :units]
    high = value.astype(jnp.bfloat16).astype(jnp.float32)
    low = value - high
    both_parts = jnp.concatenate([high, low], axis=0)
    none = jnp.zeros_like(both_parts)
    own_rows = jnp.concatenate([both_parts, none], axis=1)
    other_rows = jnp.concatenate([none, both_parts], axis=1)
    sides = jnp.concatenate([own_rows, other_rows], axis=0).astype(jnp.bfloat16)
    for copy in copies[2]:
        copy.wait()
    total = lax.dot_general(sides, down_w[...], (((1,), (1,)), ((), ())), preferred_element_type=jnp.float32)
    mp_n, _, width = out.shape[0] // 2, out.shape[1], out.shape[2]
    for side in range(2):
        sums = total[side * 32 : side * 32 + 16] + total[side * 32 + 16 : side * 32 + 32]
        for mate in range(2):
            base = mate * mp_n + (1 - h if side else h) * (mp_n // 2)
            for k in range(mp_n // 2):
                out[base + k] = sums[mate * 8 : mate * 8 + 8, k * width : (k + 1) * width]


def head_kernel(p_count, lanes, parts, residual, old_head, new_head, owner, fetched, pooled_out, message, old, new, sems):
    fetches = [pltpu.make_async_copy(old_head, old, sems.at[0]), pltpu.make_async_copy(new_head, new, sems.at[1])]
    for fetch in fetches:
        fetch.start()
    total = residual[...]
    for k in range(parts.shape[0]):
        total = total + parts[k]
    pooled = total.astype(jnp.bfloat16)
    pooled_out[...] = pooled
    for fetch in fetches:
        fetch.wait()
    of_old = jnp.dot(pooled, old[...], preferred_element_type=jnp.float32)
    of_new = jnp.dot(pooled, new[...], preferred_element_type=jnp.float32)
    row = lax.broadcasted_iota(jnp.int32, of_old.shape, 0)
    term = jnp.where(row < p_count, of_old, of_new)
    gap = jnp.zeros((term.shape[0], 128 - lanes), jnp.float32)
    pieces = [
        jnp.concatenate([term[:, k * lanes : (k + 1) * lanes], gap], axis=1) for k in range(term.shape[1] // lanes)
    ]
    negatives = jnp.zeros((owner.shape[1], 128), jnp.float32)
    for slot, mark in enumerate(marks(owner[...], fetched.shape[0])):
        negatives = negatives + lax.dot_general(
            mark.astype(jnp.bfloat16),
            fetched[:, slot, :].astype(jnp.bfloat16),
            (((0,), (0,)), ((), ())),
            preferred_element_type=jnp.float32,
        )
    rows = jnp.concatenate(pieces + [negatives], axis=0).astype(jnp.bfloat16)
    for copy in range(message.shape[0]):
        message[copy] = rows


def loss_kernel(p_count, q_count, queries, slot, messages, pooled, fresh_out, loss_out, message, held):
    n = messages.shape[0]
    rows = messages[...].astype(jnp.float32)
    total = rows[0, : n * 8]
    for k in range(1, n):
        total = total + rows[k, : n * 8]
    emb = jnp.concatenate([total[a * 8 : (a + 1) * 8] for a in range(n)], axis=1)
    fresh = emb[:p_count].astype(jnp.bfloat16).astype(jnp.float32)
    held[:p_count] = fresh
    own = held[:, pl.ds(pl.multiple_of(lax.axis_index("mp") * 128, 128), 128)]
    fresh_out[...] = own[:p_count, : fresh_out.shape[1]].astype(jnp.bfloat16)
    k_count = (rows.shape[1] - n * 8) // q_count
    loss_rows, grad_rows = [], []
    for q in range(q_count):
        query = emb[p_count + q : p_count + q + 1]
        positive = fresh[0:1]
        for k in range(1, p_count):
            positive = jnp.where(slot[q] == k, fresh[k : k + 1], positive)
        tiles = [rows[a, n * 8 + q * k_count : n * 8 + (q + 1) * k_count] for a in range(n)]
        inner = jnp.zeros((k_count, 128), jnp.float32)
        square = inner
        for a in range(n):
            inner = inner + tiles[a] * query[:, a * 128 : (a + 1) * 128]
            square = square + tiles[a] * tiles[a]
        inner = jnp.sum(inner, axis=1, keepdims=True)
        square = jnp.sum(square, axis=1, keepdims=True)
        query_norm = jnp.sqrt(jnp.sum(query * query, axis=1, keepdims=True) + 1e-06)
        below = jnp.sqrt(square + 1e-06) * query_norm * TAU
        scores = inner / below
        below_p = jnp.sqrt(jnp.sum(positive * positive, axis=1, keepdims=True) + 1e-06) * query_norm * TAU
        score_p = jnp.sum(positive * query, axis=1, keepdims=True) / below_p
        exps, exp_p = jnp.exp(scores), jnp.exp(score_p)
        total = jnp.sum(exps, axis=0, keepdims=True) + exp_p
        loss_rows.append(jnp.log(total) - score_p)
        weights = exps / total / queries
        weight_p = (exp_p / total - 1.0) / queries
        radial = (jnp.sum(weights * scores, axis=0, keepdims=True) + weight_p * score_p) / (query_norm * query_norm)
        share = weights / below
        direct = jnp.concatenate([jnp.sum(share * tile, axis=0, keepdims=True) for tile in tiles], axis=1)
        grad_rows.append(direct + (weight_p / below_p) * positive - radial * query)
    losses = jnp.concatenate(loss_rows, axis=0)
    loss_out[...] = jnp.broadcast_to(losses, loss_out.shape)
    grads = jnp.concatenate(grad_rows, axis=0).astype(jnp.bfloat16)
    width = pooled.shape[1]
    features = pooled[...].astype(jnp.float32)[p_count : p_count + q_count].astype(jnp.bfloat16)
    columns = lax.axis_size("dp")
    for k in range(message.shape[0]):
        at = k % columns * n // columns * 128
        message[k, :, :width] = features
        message[k, :, width:] = grads[:, at : at + 128]


def grad_kernel(width, arrived, out):
    block = out.shape[0]
    both = lax.dot_general(
        arrived[:, width:], arrived[:, :width], (((0,), (0,)), ((), ())), preferred_element_type=jnp.float32
    )
    shared = lax.axis_size("dp") // lax.axis_size("mp")
    chosen = both[:block]
    for k in range(1, shared):
        chosen = jnp.where(lax.axis_index("dp") % shared == k, both[k * block : (k + 1) * block], chosen)
    out[...] = chosen


def shards(
    passage_tokens,
    query_tokens,
    norm_gain,
    w_gate,
    w_up,
    w_down,
    old_head,
    new_head,
    stale_index,
    neg_owner,
    neg_row,
    pos_slot,
):
    p_count, length, width = passage_tokens.shape
    q_count, q_length, _ = query_tokens.shape
    k_count = neg_owner.shape[1]
    embed = old_head.shape[1]
    sections = lax.axis_size("section")
    shard_count = sections * lax.axis_size("dp")
    mp_n = lax.axis_size("mp")
    features = width * mp_n
    f32, bf16 = jnp.float32, jnp.bfloat16

    units = w_gate.shape[1] // 2
    cut = units // 128 * 128
    wide = -(-3 * units // 128) * 128
    rows = p_count * length + q_count * q_length
    own, other, tokens = pl.pallas_call(
        cut_kernel,
        out_shape=[jax.ShapeDtypeStruct((w_gate.shape[0], wide), bf16)] * 2
        + [jax.ShapeDtypeStruct((rows + 16, width), bf16)],
        in_specs=[in_hbm()] * 5 + [whole()],
        out_specs=[whole()] * 3,
        scratch_shapes=[pltpu.VMEM(w.shape, bf16) for w in (w_gate, w_up, w_down)] + [pltpu.SemaphoreType.DMA((5,))],
        compiler_params=params(56),
        name="cut",
    )(
        w_gate,
        w_up,
        w_down,
        passage_tokens.reshape(-1, width),
        query_tokens.reshape(-1, width),
        norm_gain[None, :],
    )
    other = half_move(other)

    request_count = q_count * k_count
    owner = neg_owner.reshape(1, request_count)
    requests = pl.pallas_call(
        ask_kernel,
        out_shape=jax.ShapeDtypeStruct((shard_count, 128), jnp.int32),
        in_specs=[whole()] * 2,
        out_specs=whole(),
        compiler_params=params(),
        name="ask",
    )(owner, neg_row.reshape(1, request_count))

    low, high = mp_move(tokens, 1, 0), mp_move(tokens, -1, 0)
    other, requests, low, high = lax.optimization_barrier((other, requests, low, high))
    gap = 6 * units - wide
    weights = along_y(jnp.pad(own, ((0, 0), (0, gap))) + jnp.pad(other, ((0, 0), (gap, 0))))

    wanted = lax.all_to_all(requests, ("section", "dp"), 0, 0, tiled=True)
    near, far, wanted = spread(tokens, low, high, wanted)
    found = pl.pallas_call(
        find_kernel,
        out_shape=jax.ShapeDtypeStruct((shard_count, 2, 128), f32),
        in_specs=[whole()] * 2,
        out_specs=whole(),
        compiler_params=params(),
        name="find",
    )(wanted, stale_index.T)
    fetched = lax.all_to_all(found, ("section", "dp"), 0, 0, tiled=True)

    normed = pl.pallas_call(
        functools.partial(norm_kernel, mp_n // 2, rows),
        out_shape=jax.ShapeDtypeStruct((2 * rows, features), bf16),
        in_specs=[whole()] * 2,
        out_specs=whole(),
        compiler_params=params(16),
        name="norm",
    )(near, far)

    pool = np.zeros((16, 2 * rows), np.float32)
    for mate in range(2):
        base = mate * rows
        for k in range(p_count):
            pool[mate * 8 + k, base + k * length : base + (k + 1) * length] = 1.0 / length
        base += p_count * length
        for k in range(q_count):
            pool[mate * 8 + p_count + k, base + k * q_length : base + (k + 1) * q_length] = 1.0 / q_length
    padded = cut + 2 * (units - cut)
    parts = pl.pallas_call(
        functools.partial(hidden_kernel, units),
        out_shape=jax.ShapeDtypeStruct((2 * mp_n, 8, width), f32),
        in_specs=[whole(), whole(), in_hbm()],
        out_specs=whole(),
        scratch_shapes=[
            pltpu.VMEM((features, 2 * units), bf16),
            pltpu.VMEM((features // 2, 2 * units), bf16),
            pltpu.VMEM((2 * rows, padded), bf16),
            pltpu.SemaphoreType.DMA((12,)),
        ],
        compiler_params=params(52),
        name="hidden",
    )(normed, jnp.asarray(pool, bf16), weights)

    groups = [[s * mp_n + m for s in (p, p + 1) for m in range(mp_n)] for p in range(0, sections, 2)]
    parts = lax.all_to_all(
        parts, ("section", "mp"), split_axis=0, concat_axis=0, axis_index_groups=groups, tiled=True
    )
    residual = jnp.concatenate(
        [
            jnp.sum(passage_tokens.astype(f32), axis=1) / length,
            jnp.sum(query_tokens.astype(f32), axis=1) / q_length,
            jnp.zeros((8 - p_count - q_count, width), f32),
        ],
        axis=0,
    )
    own_width = embed // mp_n
    message_rows = 8 * mp_n + request_count
    pooled, message = pl.pallas_call(
        functools.partial(head_kernel, p_count, own_width),
        out_shape=[
            jax.ShapeDtypeStruct((8, width), bf16),
            jax.ShapeDtypeStruct((mp_n, message_rows, 128), bf16),
        ],
        in_specs=[whole()] * 2 + [in_hbm()] * 2 + [whole()] * 2,
        out_specs=[whole()] * 2,
        scratch_shapes=[
            pltpu.VMEM((width, embed), bf16),
            pltpu.VMEM((width, embed), bf16),
            pltpu.SemaphoreType.DMA((2,)),
        ],
        compiler_params=params(),
        name="head",
    )(parts, residual, old_head, new_head, owner, fetched)
    messages = lax.all_to_all(message, "mp", 0, 0, tiled=True)

    refreshed, losses, message = pl.pallas_call(
        functools.partial(loss_kernel, p_count, q_count, q_count * shard_count),
        out_shape=[
            jax.ShapeDtypeStruct((p_count, own_width), bf16),
            jax.ShapeDtypeStruct((q_count, 128), f32),
            jax.ShapeDtypeStruct((shard_count, q_count, width + 128), bf16),
        ],
        in_specs=[pl.BlockSpec(memory_space=pltpu.SMEM)] + [whole()] * 2,
        out_specs=[whole()] * 3,
        scratch_shapes=[pltpu.VMEM((8, 128 * mp_n), f32)],
        compiler_params=params(),
        name="loss",
    )(pos_slot, messages, pooled)

    arrived = lax.all_to_all(message, ("section", "dp"), 0, 0, tiled=True)
    head_grad = pl.pallas_call(
        functools.partial(grad_kernel, width),
        out_shape=jax.ShapeDtypeStruct((embed // lax.axis_size("dp"), width), f32),
        in_specs=[whole()],
        out_specs=whole(),
        compiler_params=params(),
        name="grad",
    )(arrived.reshape(-1, width + 128)).T
    return (refreshed, losses[:, 0], head_grad)


def solution(mesh):
    placed = (
        P(("section", "dp"), None, "mp"),
        P(("section", "dp"), None, "mp"),
        P("mp"),
        P("dp", "mp"),
        P("dp", "mp"),
        P("mp", "dp"),
        P("mp", None),
        P("mp", None),
        P(("section", "dp"), "mp"),
        P(("section", "dp"), None),
        P(("section", "dp"), None),
        P(("section", "dp")),
    )
    return jax.shard_map(
        shards,
        mesh=mesh,
        in_specs=placed,
        out_specs=(P(("section", "dp"), "mp"), P(("section", "dp")), P("mp", "dp")),
        check_vma=False,
    )
```

```python
import functools
import math

import jax
import jax.numpy as jnp
import numpy as np
from jax import lax
from jax.experimental import pallas as pl
from jax.experimental.pallas import tpu as pltpu
from jax.sharding import PartitionSpec as P

TAU = 0.02
MIB = 1024 * 1024


def params(mib=8):
    return pltpu.CompilerParams(vmem_limit_bytes=mib * MIB)


def in_hbm():
    return pl.BlockSpec(memory_space=pltpu.HBM)


def whole():
    return pl.BlockSpec(memory_space=pltpu.VMEM)


def gelu(v):
    c = math.sqrt(2.0 / math.pi)
    return 0.5 * v * (1.0 + jnp.tanh(c * (v + 0.044715 * (v * v * v))))


def mp_move(block, step, flip):
    n = lax.axis_size("mp") // 2
    perm = [(x * 2 + c, ((x + step) % n) * 2 + (c ^ flip)) for x in range(n) for c in range(2)]
    return lax.ppermute(block, "mp", perm)


def mate_move(block):
    return lax.ppermute(block, "section", [(s, s ^ 1) for s in range(lax.axis_size("section"))])


def half_move(block):
    sections, shards_n = lax.axis_size("section"), lax.axis_size("dp")
    turn = sections // 2 if (sections // 2) % 2 == 0 else 0
    perm = [
        (s * shards_n + d, ((s + turn) % sections) * shards_n + (d + shards_n // 2) % shards_n)
        for s in range(sections)
        for d in range(shards_n)
    ]
    return lax.ppermute(block, ("section", "dp"), perm)


def along_y(block):
    n = lax.axis_size("dp") // 2
    groups = [[h * n + y for y in range(n)] for h in range(2)]
    return lax.all_gather(block, "dp", axis=0, axis_index_groups=groups, tiled=True)


def spread(block, low, high, wanted):
    mine = jnp.concatenate([block, low, high, mp_move(low, 1, 0)], axis=0)
    mate, wanted = lax.optimization_barrier((mate_move(mine), wanted))
    mine = jnp.concatenate([mine, mate], axis=0)
    return mine, mp_move(mine, 0, 1), wanted


def cut_kernel(gate_in, up_in, down_in, own, other, gate, up, down, sems):
    fetches = [
        pltpu.make_async_copy(source, target, sems.at[k])
        for k, (source, target) in enumerate(((gate_in, gate), (up_in, up), (down_in, down)))
    ]
    for fetch in fetches:
        fetch.start()
    units = gate.shape[1] // 2
    cut = units // 128 * 128
    gap = other.shape[1] - 3 * units
    own[:, 3 * units :] = jnp.zeros((own.shape[0], own.shape[1] - 3 * units), own.dtype)
    other[:, :gap] = jnp.zeros((own.shape[0], gap), own.dtype)
    for fetch in fetches:
        fetch.wait()
    for half in range(2):

        @pl.when(lax.axis_index("section") % 2 == half)
        def _(first=half * units):
            turned = down[first : first + units, :].astype(jnp.float32).T.astype(jnp.bfloat16)
            own[:, 2 * units : 3 * units] = turned
            other[:, gap : gap + units] = turned
            for out, base in ((own, 0), (other, gap + units)):
                out[:, base : base + cut] = gate[:, first : first + cut]
                out[:, base + cut : base + units] = gate[:, first + cut : first + units]
                out[:, base + units : base + 2 * units - cut] = up[:, first + cut : first + units]
                out[:, base + 2 * units - cut : base + 2 * units] = up[:, first : first + cut]


def norm_kernel(nx, rows, near, far, out):
    step_rows = 32
    width = near.shape[1]
    x, c = lax.axis_index("mp") // 2, lax.axis_index("mp") % 2
    parity = lax.axis_index("section") % 2
    sides = []
    for ref, core in ((near, c), (far, 1 - c)):
        for k, step in enumerate((0, -1, 1, 2)):
            place = lax.rem(x + step + nx, nx) * 2 + core
            at = pl.ds(pl.multiple_of(place * width, width), width)
            sides.append((ref, k * (rows + 16), at))
    gains = [ref[first + rows : first + rows + 1, :].astype(jnp.float32) for ref, first, _ in sides]
    for mate in range(2):
        base = mate * 4 * (rows + 16)
        target_base = (1 - parity if mate else parity) * rows

        def body(i, carry, base=base, target_base=target_base):
            start = i * step_rows
            total = jnp.zeros((step_rows, width), jnp.float32)
            for ref, first, _ in sides:
                v = ref[pl.ds(pl.multiple_of(base + first + start, 16), step_rows), :].astype(jnp.float32)
                total = total + v * v
            scale = lax.rsqrt(jnp.sum(total, axis=1, keepdims=True) / (len(sides) * width) + 1e-06)
            target = pl.ds(pl.multiple_of(target_base + start, step_rows), step_rows)
            for (ref, first, at), gain in zip(sides, gains):
                v = ref[pl.ds(pl.multiple_of(base + first + start, 16), step_rows), :].astype(jnp.float32)
                out[target, at] = (v * scale * gain).astype(jnp.bfloat16)
            return carry

        lax.fori_loop(0, rows // step_rows, body, 0)


def marks(owner, shard_n):
    count = owner.shape[1]
    hit = lax.broadcasted_iota(jnp.int32, (shard_n, count), 0) == owner
    place = lax.broadcasted_iota(jnp.int32, (shard_n, count), 1).astype(jnp.float32)
    first = jnp.min(jnp.where(hit, place, 2.0 * count), axis=1, keepdims=True)
    last = jnp.max(jnp.where(hit, place, -1.0), axis=1, keepdims=True)
    return jnp.where(hit & (place == first), 1.0, 0.0), jnp.where(hit & (place == last) & (last > first), 1.0, 0.0)


def ask_kernel(owner, row, out):
    first, second = marks(owner[...], out.shape[0])
    wanted = row[...].astype(jnp.float32)
    one = jnp.sum(first * wanted, axis=1, keepdims=True)
    two = jnp.sum(second * wanted, axis=1, keepdims=True)
    lane = lax.broadcasted_iota(jnp.int32, out.shape, 1)
    out[...] = jnp.where(lane == 0, one, jnp.where(lane == 1, two, 0.0)).astype(jnp.int32)


def find_kernel(wanted, index, out):
    width, count = index.shape
    row = lax.broadcasted_iota(jnp.int32, (wanted.shape[0], count), 1)
    gap = jnp.zeros((wanted.shape[0], 128 - width), jnp.float32)
    for slot in range(2):
        hit = jnp.where(row == wanted[:, slot : slot + 1], 1.0, 0.0).astype(jnp.bfloat16)
        found = lax.dot_general(hit, index[...], (((1,), (1,)), ((), ())), preferred_element_type=jnp.float32)
        out[:, slot, :] = jnp.concatenate([found, gap], axis=1)


def hidden_kernel(units, normed, pool, weights, out, up_w, down_w, hidden, sems):
    h = lax.axis_index("dp") // (lax.axis_size("dp") // 2)
    rows = weights.shape[0]
    parts = 4
    piece = rows // parts
    copies = []
    for side, target in ((0, up_w), (2, up_w), (1, down_w)):
        base = rows if side == 2 else 0
        copies.append(
            [
                pltpu.make_async_copy(
                    weights.at[pl.ds(k * piece, piece), pl.ds(2 * units * side, 2 * units)],
                    target.at[pl.ds(base + k * piece, piece), :],
                    sems.at[side * parts + k],
                )
                for k in range(parts)
            ]
        )
    for group in copies:
        for copy in group:
            copy.start()
    cut = units // 128 * 128
    tail = units - cut
    tokens = normed.shape[0] // 2
    for part in range(2):
        at = slice(part * tokens, (part + 1) * tokens)
        both = None
        for side in range(2):
            if part == 0:
                for copy in copies[side]:
                    copy.wait()
            columns = pl.ds(pl.multiple_of((1 - h if side else h) * rows, rows), rows)
            term = jnp.dot(
                normed[at, columns], up_w[side * rows : (side + 1) * rows, :], preferred_element_type=jnp.float32
            )
            both = term if both is None else both + term
        hidden[at, :cut] = (gelu(both[:, :cut]) * both[:, 2 * units - cut :]).astype(jnp.bfloat16)
        if tail:
            edge = both[:, cut : cut + 2 * tail]
            hidden[at, cut : cut + 2 * tail] = (gelu(edge) * pltpu.roll(edge, tail, 1)).astype(jnp.bfloat16)
    value = jnp.dot(pool[...], hidden[...], preferred_element_type=jnp.float32)[:, :units]
    high = value.astype(jnp.bfloat16).astype(jnp.float32)
    low = value - high
    both_parts = jnp.concatenate([high, low], axis=0)
    none = jnp.zeros_like(both_parts)
    own_rows = jnp.concatenate([both_parts, none], axis=1)
    other_rows = jnp.concatenate([none, both_parts], axis=1)
    sides = jnp.concatenate([own_rows, other_rows], axis=0).astype(jnp.bfloat16)
    for copy in copies[2]:
        copy.wait()
    total = lax.dot_general(sides, down_w[...], (((1,), (1,)), ((), ())), preferred_element_type=jnp.float32)
    mp_n, _, width = out.shape[0] // 2, out.shape[1], out.shape[2]
    for side in range(2):
        sums = total[side * 32 : side * 32 + 16] + total[side * 32 + 16 : side * 32 + 32]
        for mate in range(2):
            base = mate * mp_n + (1 - h if side else h) * (mp_n // 2)
            for k in range(mp_n // 2):
                out[base + k] = sums[mate * 8 : mate * 8 + 8, k * width : (k + 1) * width]


def head_kernel(p_count, lanes, parts, residual, old_head, new_head, owner, fetched, pooled_out, message, old, new, sems):
    fetches = [pltpu.make_async_copy(old_head, old, sems.at[0]), pltpu.make_async_copy(new_head, new, sems.at[1])]
    for fetch in fetches:
        fetch.start()
    total = residual[...]
    for k in range(parts.shape[0]):
        total = total + parts[k]
    pooled = total.astype(jnp.bfloat16)
    pooled_out[...] = pooled
    for fetch in fetches:
        fetch.wait()
    of_old = jnp.dot(pooled, old[...], preferred_element_type=jnp.float32)
    of_new = jnp.dot(pooled, new[...], preferred_element_type=jnp.float32)
    row = lax.broadcasted_iota(jnp.int32, of_old.shape, 0)
    term = jnp.where(row < p_count, of_old, of_new)
    gap = jnp.zeros((term.shape[0], 128 - lanes), jnp.float32)
    pieces = [
        jnp.concatenate([term[:, k * lanes : (k + 1) * lanes], gap], axis=1) for k in range(term.shape[1] // lanes)
    ]
    negatives = jnp.zeros((owner.shape[1], 128), jnp.float32)
    for slot, mark in enumerate(marks(owner[...], fetched.shape[0])):
        negatives = negatives + lax.dot_general(
            mark.astype(jnp.bfloat16),
            fetched[:, slot, :].astype(jnp.bfloat16),
            (((0,), (0,)), ((), ())),
            preferred_element_type=jnp.float32,
        )
    rows = jnp.concatenate(pieces + [negatives], axis=0).astype(jnp.bfloat16)
    for copy in range(message.shape[0]):
        message[copy] = rows


def loss_kernel(p_count, q_count, queries, slot, messages, pooled, fresh_out, loss_out, message, held):
    n = messages.shape[0]
    rows = messages[...].astype(jnp.float32)
    total = rows[0, : n * 8]
    for k in range(1, n):
        total = total + rows[k, : n * 8]
    emb = jnp.concatenate([total[a * 8 : (a + 1) * 8] for a in range(n)], axis=1)
    fresh = emb[:p_count].astype(jnp.bfloat16).astype(jnp.float32)
    held[:p_count] = fresh
    own = held[:, pl.ds(pl.multiple_of(lax.axis_index("mp") * 128, 128), 128)]
    fresh_out[...] = own[:p_count, : fresh_out.shape[1]].astype(jnp.bfloat16)
    k_count = (rows.shape[1] - n * 8) // q_count
    def each(parts):
        return jnp.concatenate([jnp.broadcast_to(v, (k_count, v.shape[1])) for v in parts], axis=0)

    def groups(values):
        return [
            jnp.sum(values[q * k_count : (q + 1) * k_count], axis=0, keepdims=True) for q in range(q_count)
        ]

    own_queries = [emb[p_count + q : p_count + q + 1] for q in range(q_count)]
    positives = []
    for q in range(q_count):
        positive = fresh[0:1]
        for k in range(1, p_count):
            positive = jnp.where(slot[q] == k, fresh[k : k + 1], positive)
        positives.append(positive)
    query, positive = each(own_queries), each(positives)
    cands = jnp.concatenate([rows[a, n * 8 :] for a in range(n)], axis=1)
    query_norm = jnp.sqrt(jnp.sum(query * query, axis=1, keepdims=True) + 1e-06)
    below = jnp.sqrt(jnp.sum(cands * cands, axis=1, keepdims=True) + 1e-06) * query_norm * TAU
    scores = jnp.sum(cands * query, axis=1, keepdims=True) / below
    below_p = jnp.sqrt(jnp.sum(positive * positive, axis=1, keepdims=True) + 1e-06) * query_norm * TAU
    score_p = jnp.sum(positive * query, axis=1, keepdims=True) / below_p
    exps, exp_p = jnp.exp(scores), jnp.exp(score_p)
    total = each(groups(exps)) + exp_p
    losses = jnp.log(total) - score_p
    weights = exps / total / queries
    weight_p = (exp_p / total - 1.0) / queries
    radial = (each(groups(weights * scores)) + weight_p * score_p) / (query_norm * query_norm)
    direct = groups((weights / below) * cands)
    scale_p = weight_p / below_p
    grad_rows = []
    for q in range(q_count):
        at = slice(q * k_count, q * k_count + 1)
        grad_rows.append(direct[q] + scale_p[at] * positives[q] - radial[at] * own_queries[q])
        loss_out[q : q + 1, :] = jnp.broadcast_to(losses[at], (1, loss_out.shape[1]))
    grads = jnp.concatenate(grad_rows, axis=0).astype(jnp.bfloat16)
    width = pooled.shape[1]
    features = pooled[...].astype(jnp.float32)[p_count : p_count + q_count].astype(jnp.bfloat16)
    columns = lax.axis_size("dp")
    for k in range(message.shape[0]):
        at = k % columns * n // columns * 128
        message[k, :, :width] = features
        message[k, :, width:] = grads[:, at : at + 128]


def grad_kernel(width, arrived, out):
    block = out.shape[0]
    both = lax.dot_general(
        arrived[:, width:], arrived[:, :width], (((0,), (0,)), ((), ())), preferred_element_type=jnp.float32
    )
    shared = lax.axis_size("dp") // lax.axis_size("mp")
    chosen = both[:block]
    for k in range(1, shared):
        chosen = jnp.where(lax.axis_index("dp") % shared == k, both[k * block : (k + 1) * block], chosen)
    out[...] = chosen


def shards(
    passage_tokens,
    query_tokens,
    norm_gain,
    w_gate,
    w_up,
    w_down,
    old_head,
    new_head,
    stale_index,
    neg_owner,
    neg_row,
    pos_slot,
):
    p_count, length, width = passage_tokens.shape
    q_count, q_length, _ = query_tokens.shape
    k_count = neg_owner.shape[1]
    embed = old_head.shape[1]
    sections = lax.axis_size("section")
    shard_count = sections * lax.axis_size("dp")
    mp_n = lax.axis_size("mp")
    features = width * mp_n
    f32, bf16 = jnp.float32, jnp.bfloat16

    units = w_gate.shape[1] // 2
    cut = units // 128 * 128
    wide = -(-3 * units // 128) * 128
    own, other = pl.pallas_call(
        cut_kernel,
        out_shape=[jax.ShapeDtypeStruct((w_gate.shape[0], lanes), bf16) for lanes in (6 * units, wide)],
        in_specs=[in_hbm()] * 3,
        out_specs=[whole()] * 2,
        scratch_shapes=[pltpu.VMEM(w.shape, bf16) for w in (w_gate, w_up, w_down)] + [pltpu.SemaphoreType.DMA((3,))],
        compiler_params=params(56),
        name="cut",
    )(w_gate, w_up, w_down)
    other = half_move(other)

    rows = p_count * length + q_count * q_length
    gain_rows = jnp.broadcast_to(norm_gain[None, :], (16, width))
    tokens = jnp.concatenate(
        [passage_tokens.reshape(-1, width), query_tokens.reshape(-1, width), gain_rows], axis=0
    )
    request_count = q_count * k_count
    owner = neg_owner.reshape(1, request_count)
    requests = pl.pallas_call(
        ask_kernel,
        out_shape=jax.ShapeDtypeStruct((shard_count, 128), jnp.int32),
        in_specs=[whole()] * 2,
        out_specs=whole(),
        compiler_params=params(),
        name="ask",
    )(owner, neg_row.reshape(1, request_count))

    low, high = mp_move(tokens, 1, 0), mp_move(tokens, -1, 0)
    other, requests, low = lax.optimization_barrier((other, requests, low))
    edge = 6 * units - wide
    weights = along_y(lax.dynamic_update_slice(own, own[:, edge:] + other, (0, edge)))

    wanted = lax.all_to_all(requests, ("section", "dp"), 0, 0, tiled=True)
    near, far, wanted = spread(tokens, low, high, wanted)
    found = pl.pallas_call(
        find_kernel,
        out_shape=jax.ShapeDtypeStruct((shard_count, 2, 128), f32),
        in_specs=[whole()] * 2,
        out_specs=whole(),
        compiler_params=params(),
        name="find",
    )(wanted, stale_index.T)
    fetched = lax.all_to_all(found, ("section", "dp"), 0, 0, tiled=True)

    normed = pl.pallas_call(
        functools.partial(norm_kernel, mp_n // 2, rows),
        out_shape=jax.ShapeDtypeStruct((2 * rows, features), bf16),
        in_specs=[whole()] * 2,
        out_specs=whole(),
        compiler_params=params(16),
        name="norm",
    )(near, far)

    pool = np.zeros((16, 2 * rows), np.float32)
    for mate in range(2):
        base = mate * rows
        for k in range(p_count):
            pool[mate * 8 + k, base + k * length : base + (k + 1) * length] = 1.0 / length
        base += p_count * length
        for k in range(q_count):
            pool[mate * 8 + p_count + k, base + k * q_length : base + (k + 1) * q_length] = 1.0 / q_length
    padded = cut + 2 * (units - cut)
    parts = pl.pallas_call(
        functools.partial(hidden_kernel, units),
        out_shape=jax.ShapeDtypeStruct((2 * mp_n, 8, width), f32),
        in_specs=[whole(), whole(), in_hbm()],
        out_specs=whole(),
        scratch_shapes=[
            pltpu.VMEM((features, 2 * units), bf16),
            pltpu.VMEM((features // 2, 2 * units), bf16),
            pltpu.VMEM((2 * rows, padded), bf16),
            pltpu.SemaphoreType.DMA((12,)),
        ],
        compiler_params=params(52),
        name="hidden",
    )(normed, jnp.asarray(pool, bf16), weights)

    groups = [[s * mp_n + m for s in (p, p + 1) for m in range(mp_n)] for p in range(0, sections, 2)]
    parts = lax.all_to_all(
        parts, ("section", "mp"), split_axis=0, concat_axis=0, axis_index_groups=groups, tiled=True
    )
    residual = jnp.concatenate(
        [
            jnp.sum(passage_tokens.astype(f32), axis=1) / length,
            jnp.sum(query_tokens.astype(f32), axis=1) / q_length,
            jnp.zeros((8 - p_count - q_count, width), f32),
        ],
        axis=0,
    )
    own_width = embed // mp_n
    message_rows = 8 * mp_n + request_count
    pooled, message = pl.pallas_call(
        functools.partial(head_kernel, p_count, own_width),
        out_shape=[
            jax.ShapeDtypeStruct((8, width), bf16),
            jax.ShapeDtypeStruct((mp_n, message_rows, 128), bf16),
        ],
        in_specs=[whole()] * 2 + [in_hbm()] * 2 + [whole()] * 2,
        out_specs=[whole()] * 2,
        scratch_shapes=[
            pltpu.VMEM((width, embed), bf16),
            pltpu.VMEM((width, embed), bf16),
            pltpu.SemaphoreType.DMA((2,)),
        ],
        compiler_params=params(),
        name="head",
    )(parts, residual, old_head, new_head, owner, fetched)
    messages = lax.all_to_all(message, "mp", 0, 0, tiled=True)

    refreshed, losses, message = pl.pallas_call(
        functools.partial(loss_kernel, p_count, q_count, q_count * shard_count),
        out_shape=[
            jax.ShapeDtypeStruct((p_count, own_width), bf16),
            jax.ShapeDtypeStruct((q_count, 128), f32),
            jax.ShapeDtypeStruct((shard_count, q_count, width + 128), bf16),
        ],
        in_specs=[pl.BlockSpec(memory_space=pltpu.SMEM)] + [whole()] * 2,
        out_specs=[whole()] * 3,
        scratch_shapes=[pltpu.VMEM((8, 128 * mp_n), f32)],
        compiler_params=params(),
        name="loss",
    )(pos_slot, messages, pooled)

    arrived = lax.all_to_all(message, ("section", "dp"), 0, 0, tiled=True)
    head_grad = pl.pallas_call(
        functools.partial(grad_kernel, width),
        out_shape=jax.ShapeDtypeStruct((embed // lax.axis_size("dp"), width), f32),
        in_specs=[whole()],
        out_specs=whole(),
        compiler_params=params(),
        name="grad",
    )(arrived.reshape(-1, width + 128)).T
    return (refreshed, losses[:, 0], head_grad)


def solution(mesh):
    placed = (
        P(("section", "dp"), None, "mp"),
        P(("section", "dp"), None, "mp"),
        P("mp"),
        P("dp", "mp"),
        P("dp", "mp"),
        P("mp", "dp"),
        P("mp", None),
        P("mp", None),
        P(("section", "dp"), "mp"),
        P(("section", "dp"), None),
        P(("section", "dp"), None),
        P(("section", "dp")),
    )
    return jax.shard_map(
        shards,
        mesh=mesh,
        in_specs=placed,
        out_specs=(P(("section", "dp"), "mp"), P(("section", "dp")), P("mp", "dp")),
        check_vma=False,
    )
```
